512 devices in a mesh: gx: 16 (over z), gy: 16 (over y, x), gz: 2 (over core).
Axes of the slice: x: 4, y: 4, z: 16, core: 2. Of those that a mesh axis runs over, the one named last changes fastest.
Arguments:
- fields: float32 [4, 16, 768, 2048], P(None, 'gz', 'gx', 'gy'), may hold values from -6 to 6
Outputs:
- details_one: float32 [7, 4, 8, 384, 1024], P(None, 'gz', None, 'gx', 'gy')
- details_two: float32 [7, 4, 4, 192, 512], P(None, 'gz', None, 'gx', 'gy')
- details_three: float32 [7, 4, 2, 96, 256], P(None, 'gz', None, 'gx', 'gy')
- details_four: float32 [7, 4, 1, 48, 128], P(None, 'gz', None, 'gx', 'gy')
- coarsest: float32 [4, 1, 48, 128], P('gz', None, 'gx', 'gy')
The draws below stay inside these ranges and needn't reach their ends.
All inputs are finite; a program needn't handle non-finite values.
Results may differ from the reference program's by a relative error of at most 0.000027.
Values sent between devices are 32-bit elements; how exact they have to be, the bound alone decides.
A program may use at most 64 MiB of HBM per device.

```python
import jax
import jax.numpy as jnp
from jax import lax

V = 4
LEVELS = 4
Z = 16
X = 768
Y = 2048


def level_of(rng, shape, split, smallest, high):
    def one(dim, blocks):
        heights = jax.random.uniform(jax.random.fold_in(jax.random.fold_in(rng, 6), dim), (blocks,), jnp.float32, smallest / len(split), high / len(split))
        return jnp.repeat(jnp.exp(heights), shape[dim] // blocks).reshape((-1,) + (1,) * (len(shape) - dim - 1))

    loudness = one(*split[0])
    for cut in split[1:]:
        loudness = loudness * one(*cut)
    return loudness


def gaussian(stream_key, shape, spread, limit, pieces=(), dtype=jnp.bfloat16):
    entries = spread * jax.random.normal(stream_key, shape, jnp.float32)
    if pieces:
        entries = entries * level_of(stream_key, shape, pieces, -0.22, 0.18)
    return jnp.clip(entries, -limit, limit).astype(dtype)


def setup_inputs(seed: int = 0) -> dict:
    streams_of = jax.random.split(jax.random.key(seed), 2)
    return {
        "fields": gaussian(streams_of[0], (V, Z, X, Y), 1.0, 6.0, ((1, 2), (2, 16), (3, 16)), jnp.float32),
    }


lift_alpha = -1.586134342059924
lift_beta = -0.052980118572961
lift_gamma = 0.882911075530934
lift_delta = 0.443506852043971
scale_low = 0.869864451624781
scale_high = 1.149604398860241


def window_slice(values, start, stop, dimension):
    return lax.slice_in_dim(values, start, stop, 1, dimension)


def lift_extended(extended, dimension):
    even_part = lax.slice_in_dim(extended, 0, None, 2, dimension)
    odd_part = lax.slice_in_dim(extended, 1, None, 2, dimension)
    halves = even_part.shape[dimension]
    step_one = window_slice(odd_part, 0, halves - 1, dimension) + lift_alpha * (
        window_slice(even_part, 0, halves - 1, dimension) + window_slice(even_part, 1, halves, dimension))
    step_two = window_slice(even_part, 1, halves - 1, dimension) + lift_beta * (
        window_slice(step_one, 0, halves - 2, dimension) + window_slice(step_one, 1, halves - 1, dimension))
    step_three = window_slice(step_one, 1, halves - 2, dimension) + lift_gamma * (
        window_slice(step_two, 0, halves - 3, dimension) + window_slice(step_two, 1, halves - 2, dimension))
    step_four = window_slice(step_two, 1, halves - 3, dimension) + lift_delta * (
        window_slice(step_three, 0, halves - 4, dimension) + window_slice(step_three, 1, halves - 3, dimension))
    return step_four * scale_low, window_slice(step_three, 1, halves - 3, dimension) * scale_high


def lift_periodic(values, dimension):
    extent = values.shape[dimension]
    repeats = (4 + extent - 1) // extent
    tiled = jnp.concatenate([values] * (2 * repeats + 1), axis=dimension)
    extended = window_slice(tiled, repeats * extent - 4, repeats * extent + extent + 4, dimension)
    return lift_extended(extended, dimension)


def one_level(approx):
    low_band, high_band = lift_periodic(approx, 2)
    paired = jnp.stack([low_band, high_band], 0)
    low_band, high_band = lift_periodic(paired, 4)
    quartet = jnp.stack([low_band, high_band], 0)
    low_band, high_band = lift_periodic(quartet, 3)
    octet = jnp.stack([low_band, high_band], 0)
    octet = octet.reshape((8,) + octet.shape[3:])
    return octet[0], octet[1:]


def transform_one(single):
    approx = single
    details = []
    for level_index in range(LEVELS):
        approx, bands = one_level(approx)
        details.append(bands)
    return details, approx


def reference(fields):
    detail_lists = [[] for level_index in range(LEVELS)]
    coarse_list = []
    for variable in range(V):
        details, approx = transform_one(fields[variable:variable + 1])
        for level_index in range(LEVELS):
            detail_lists[level_index].append(details[level_index])
        coarse_list.append(approx)
    stacked = [jnp.concatenate(items, axis=1) for items in detail_lists]
    return stacked[0], stacked[1], stacked[2], stacked[3], jnp.concatenate(coarse_list, axis=0)
```

```python
import functools

import jax
import jax.numpy as jnp
import numpy as np
from jax import lax
from jax.experimental import pallas as pl
from jax.experimental.pallas import tpu as pltpu
from jax.sharding import PartitionSpec as P

MESH = pl.DeviceIdType.MESH
LEVELS = 4
NX, NY, NZ = 48, 128, 8

lift_alpha = -1.586134342059924
lift_beta = -0.052980118572961
lift_gamma = 0.882911075530934
lift_delta = 0.443506852043971
scale_low = 0.869864451624781
scale_high = 1.149604398860241


def lift_halves(even, odd, up, down):
    one = odd + lift_alpha * (even + up(even))
    two = even + lift_beta * (down(one) + one)
    three = one + lift_gamma * (two + up(two))
    four = two + lift_delta * (down(three) + three)
    return four * scale_low, three * scale_high


def operators(extent):
    tiles = 9
    line = np.zeros((tiles * extent, extent))
    line[4 * extent : 5 * extent] = np.eye(extent)
    found = []
    for level in range(LEVELS):
        low, high = lift_halves(
            line[0::2], line[1::2], lambda a: np.roll(a, -1, 0), lambda a: np.roll(a, 1, 0)
        )
        count = extent >> (level + 1)
        start = 4 * count
        pair = []
        for band in (low, high):
            rows = {}
            for k in range(band.shape[0]):
                if np.any(band[k]):
                    rows[k - start] = band[k]
            pair.append(rows)
        found.append(pair)
        line = low
    return found


ROWS_X = operators(NX)
ROWS_Y = operators(NY)
PAD_X = (24, 16, 8, 8)
PLANES = (32, 16, 8, 4)


def split_rows(pair, count):
    groups = {"own": [], "left": [], "right": [], "far": []}
    for band, rows in enumerate(pair):
        for k in sorted(rows):
            if k < -count or k >= 2 * count + 1:
                raise ValueError
            name = "left" if k < 0 else "own" if k < count else "right" if k < 2 * count else "far"
            groups[name].append((band, k, rows[k]))
    return groups


GX = [split_rows(ROWS_X[i], NX >> (i + 1)) for i in range(LEVELS)]
GY = [split_rows(ROWS_Y[i], NY >> (i + 1)) for i in range(LEVELS)]


def x_own(level):
    m = np.zeros((2 * PAD_X[level], NX), np.float32)
    for band, k, w in GX[level]["own"]:
        m[band * PAD_X[level] + k] = w
    return m


def x_edge(level):
    if level == 0:
        m = np.zeros((16, 2 * NX), np.float32)
        for side, name in enumerate(("left", "right")):
            for i, (_, _, w) in enumerate(GX[0][name]):
                for v in range(2):
                    m[8 * side + 4 * v + i, v * NX : (v + 1) * NX] = w
        return m
    m = np.zeros((16, NX), np.float32)
    for side, name in enumerate(("left", "right")):
        rows = list(GX[level][name])
        if side:
            rows = rows + GX[level]["far"]
        for i, (_, _, w) in enumerate(rows):
            m[8 * side + i] = w
    return m


def y_own(level, stride):
    m = np.zeros((NY, 2 * stride), np.float32)
    for band, k, w in GY[level]["own"]:
        m[:, band * stride + k] = w
    return m


def y_edge(level):
    m = np.zeros((16, NY), np.float32)
    for side, name in enumerate(("left", "right")):
        for i, (_, _, w) in enumerate(GY[level][name]):
            m[8 * side + i] = w
    return m


def y_place(level, stride):
    count = NY >> (level + 1)
    m = np.zeros((16, 2 * stride), np.float32)
    for side, name in enumerate(("left", "right")):
        for i, (band, k, _) in enumerate(GY[level][name]):
            m[8 * side + i, band * stride + (k + count if side == 0 else k - count)] = 1
    return m


assert not any(GY[i]["far"] for i in range(LEVELS))

X_OWN = [x_own(i) for i in range(LEVELS)]
X_EDGE = [x_edge(i) for i in range(LEVELS)]
Y_OWN = [y_own(i, 128) for i in range(LEVELS)]
Y_PACK = [y_own(i, 64) for i in range(LEVELS)]
Y_EDGE = [y_edge(i) for i in range(LEVELS)]
Y_PLACE = [y_place(i, 128) for i in range(LEVELS)]
Y_PLACE_PACK = [y_place(i, 64) for i in range(LEVELS)]
GROUPS = (X_OWN, X_EDGE, Y_OWN, Y_PACK, Y_EDGE, Y_PLACE, Y_PLACE_PACK)
CONSTANTS = [m for group in GROUPS for m in group]

EDGE_AT = (0, 128, 256, 320)
EDGE_ROWS = (128, 128, 64, 32)
OWN_AT = (0, 1536, 2048, 2176)
OWN_ROWS = tuple(2 * PLANES[i] * PAD_X[i] for i in range(LEVELS))


def exact(a, b):
    return jnp.dot(a, b, precision=lax.Precision.HIGHEST, preferred_element_type=jnp.float32)


def exact_nt(a, b):
    return lax.dot_general(
        a, b, (((1,), (1,)), ((), ())), precision=lax.Precision.HIGHEST, preferred_element_type=jnp.float32
    )


def exact_tn(a, b):
    return lax.dot_general(
        a, b, (((0,), (0,)), ((), ())), precision=lax.Precision.HIGHEST, preferred_element_type=jnp.float32
    )


def stacked(wide, planes):
    return jnp.concatenate([wide[:, 128 * p : 128 * (p + 1)] for p in range(planes)], axis=0)


def kernel(ring_x, ring_y, *refs):
    fields = refs[0]
    n = len(CONSTANTS)
    table = [refs[1 + 4 * g : 5 + 4 * g] for g in range(len(GROUPS))]
    x_own_, x_edge_, y_own_, y_pack_, y_edge_, y_place_, y_place_pack_ = table
    outs = refs[1 + n : 6 + n]
    (raw, wide1, wide2, wide3, wide4, v1, v2, v3, v4, m_out, c_out, k_out,
     m_in, c_in, k_in, far_m, far_k, send, recv, local) = refs[6 + n :]
    wides = (wide1, wide2, wide3, wide4)
    values = (v1, v2, v3, v4)

    gx, gy, gz = lax.axis_index("gx"), lax.axis_index("gy"), lax.axis_index("gz")

    def at(dx, dy):
        return (lax.rem(gx + dx + ring_x, ring_x), lax.rem(gy + dy + ring_y, ring_y), gz)

    partner = (gx, gy, 1 - gz)
    near = [(dx, dy) for dx in (-1, 0, 1) for dy in (-1, 0, 1) if dx or dy]
    barrier = pltpu.get_barrier_semaphore()
    for d in near + [(-2, -1), (-2, 0), (-2, 1)]:
        pl.semaphore_signal(barrier, inc=1, device_id=at(*d), device_id_type=MESH)
    pl.semaphore_signal(barrier, inc=1, device_id=partner, device_id_type=MESH)
    keep = pltpu.make_async_copy(fields.at[pl.ds(2 * gz, 2)], raw.at[:, pl.ds(NZ * gz, NZ)], local)
    keep.start()
    pl.semaphore_wait(barrier, 12)

    def copy(src, dst, slot, device):
        c = pltpu.make_async_remote_copy(
            src_ref=src, dst_ref=dst, send_sem=send.at[slot], recv_sem=recv.at[slot],
            device_id=device, device_id_type=MESH,
        )
        c.start()
        return c

    swap = copy(fields.at[pl.ds(2 - 2 * gz, 2)], raw.at[:, pl.ds(NZ * gz, NZ)], 0, partner)
    keep.wait()
    swap.wait()

    for v in range(2):
        planes = [raw[v, i] for i in range(2 * NZ)]
        for level in range(LEVELS):
            half = len(planes) // 2
            even, odd = planes[0::2], planes[1::2]
            one = [odd[k] + lift_alpha * (even[k] + even[(k + 1) % half]) for k in range(half)]
            two = [even[k] + lift_beta * (one[k - 1] + one[k]) for k in range(half)]
            three = [one[k] + lift_gamma * (two[k] + two[(k + 1) % half]) for k in range(half)]
            four = [two[k] + lift_delta * (three[k - 1] + three[k]) for k in range(half)]
            low = [a * scale_low for a in four]
            high = [a * scale_high for a in three]
            for i, plane in enumerate(low + high):
                if level == 0:
                    wide1[NX * v : NX * (v + 1), 128 * i : 128 * (i + 1)] = plane
                else:
                    j = v * 2 * half + i
                    wides[level][:, 128 * j : 128 * (j + 1)] = plane
            planes = low

    copies = []
    for level in range(LEVELS):
        edge = exact(x_edge_[level][...], wides[level][...])
        lanes = 16 if level == 0 else PLANES[level]
        first, count = EDGE_AT[level], EDGE_ROWS[level]
        for side in range(2):
            rows = stacked(edge[8 * side : 8 * side + 8], lanes)
            m_out[side, first : first + count, :] = exact(rows, y_pack_[level][...])
            corner = exact_nt(y_edge_[level][...], rows)
            k_out[side, :, :, first : first + count] = corner.reshape(2, 8, count)
    for side, dx in ((0, -1), (1, 1)):
        copies.append(copy(m_out.at[side], m_in.at[side], 1 + side, at(dx, 0)))
        for up, dy in ((0, -1), (1, 1)):
            copies.append(copy(k_out.at[side, up], k_in.at[side, up], 3 + 2 * side + up, at(dx, dy)))
    copies.append(copy(m_out.at[1, pl.ds(320, 32)], far_m, 7, at(2, 0)))
    for up, dy in ((0, -1), (1, 1)):
        copies.append(copy(k_out.at[1, up, :, pl.ds(256, 128)], far_k.at[up], 8 + up, at(2, dy)))

    tall = []
    for level in range(LEVELS):
        pad, p = PAD_X[level], PLANES[level]
        if level == 0:
            pieces = [exact(x_own_[0][...], wide1[NX * v : NX * (v + 1), :]) for v in range(2)]
            both = jnp.concatenate(pieces, axis=1)
        else:
            both = exact(x_own_[level][...], wides[level][...])
        rows = jnp.concatenate([stacked(both[:pad], p), stacked(both[pad:], p)], axis=0)
        first, count = OWN_AT[level], OWN_ROWS[level]
        c_out[:, :, first : first + count] = exact_nt(y_edge_[level][...], rows).reshape(2, 8, count)
        tall.append(rows)
    for up, dy in ((0, -1), (1, 1)):
        copies.append(copy(c_out.at[up], c_in.at[up], 10 + up, at(0, dy)))
    for level in range(LEVELS):
        pad, p = PAD_X[level], PLANES[level]
        done = exact(tall[level], y_own_[level][...])
        for by in range(2):
            values[level][by] = done[:, 128 * by : 128 * by + 128].reshape(2, p, pad, 128)

    for c in copies:
        c.wait()

    row = lax.broadcasted_iota(jnp.int32, (1, 8, 128), 1)

    def shifted(block, start, count, to):
        turn = (to - start) % 8
        if turn:
            block = pltpu.roll(block, turn, 1)
        return jnp.where((row >= to) & (row < to + count), block, 0.0)

    for level in range(LEVELS):
        pad, p = PAD_X[level], PLANES[level]
        count_x = NX >> (level + 1)
        first, count = OWN_AT[level], OWN_ROWS[level]
        c = c_in[:, :, first : first + count].reshape(16, count)
        more = exact_tn(c, y_place_[level][...])
        for by in range(2):
            values[level][by] += more[:, 128 * by : 128 * by + 128].reshape(2, p, pad, 128)
        first, count = EDGE_AT[level], EDGE_ROWS[level]
        for side in range(2):
            k = k_in[side, :, :, first : first + count].reshape(16, count)
            m = m_in[side, first : first + count, :] + exact_tn(k, y_place_pack_[level][...])
            if level == 3 and side == 1:
                k = far_k[:, :, 64:96].reshape(16, count)
                far = far_m[...] + exact_tn(k, y_place_pack_[level][...])
            for by in range(2):
                turned = m if by == 0 else pltpu.roll(m, 64, 1)
                block = turned.reshape(count // 8, 8, 128)
                for bx in range(2):
                    hits = [i for i, h in enumerate(GX[level]["right" if side else "left"]) if h[0] == bx]
                    k0 = GX[level]["right" if side else "left"][hits[0]][1]
                    to = k0 - count_x if side else k0 + count_x
                    base = to - to % 8
                    if level == 0:
                        for v in range(2):
                            add = shifted(block, hits[0] + 4 * v, len(hits), to - base)
                            values[0][by, bx, 16 * v : 16 * v + 16, base : base + 8, :] += add
                    else:
                        add = shifted(block, hits[0], len(hits), to - base)
                        if level == 3 and side == 1 and bx == 0:
                            ft = far if by == 0 else pltpu.roll(far, 64, 1)
                            add = add + shifted(ft.reshape(count // 8, 8, 128), 6, 1, 0)
                        values[level][by, bx, :, base : base + 8, :] += add

    for level in range(LEVELS):
        half = 8 >> level
        rows, columns = NX >> (level + 1), NY >> (level + 1)
        for b in range(8):
            bz, by, bx = b // 4, b // 2 % 2, b % 2
            if b == 0 and level < 3:
                continue
            for v in range(2):
                j = (2 * v + bz) * half
                got = values[level][by, bx, j : j + half, :rows, :columns]
                if b == 0:
                    outs[4][v] = got
                else:
                    outs[level][b - 1, v] = got


def solution(mesh):
    ring_x, ring_y = mesh.shape["gx"], mesh.shape["gy"]
    shapes = [(7, 2, 8 >> i, NX >> (i + 1), NY >> (i + 1)) for i in range(LEVELS)]
    shapes.append((2, 1, NX >> LEVELS, NY >> LEVELS))
    f32 = jnp.float32

    def body(fields):
        return tuple(
            pl.pallas_call(
                functools.partial(kernel, ring_x, ring_y),
                out_shape=[jax.ShapeDtypeStruct(s, f32) for s in shapes],
                in_specs=[pl.BlockSpec(memory_space=pl.ANY)]
                + [pl.BlockSpec(memory_space=pltpu.VMEM)] * len(CONSTANTS),
                out_specs=[pl.BlockSpec(memory_space=pltpu.VMEM)] * 5,
                scratch_shapes=[
                    pltpu.VMEM((2, 2 * NZ, NX, NY), f32),
                    pltpu.VMEM((2 * NX, 16 * NY), f32),
                    pltpu.VMEM((NX, 16 * NY), f32),
                    pltpu.VMEM((NX, 8 * NY), f32),
                    pltpu.VMEM((NX, 4 * NY), f32),
                ]
                + [pltpu.VMEM((2, 2, PLANES[i], PAD_X[i], 128), f32) for i in range(LEVELS)]
                + [pltpu.VMEM((2, 352, 128), f32), pltpu.VMEM((2, 8, 2304), f32), pltpu.VMEM((2, 2, 8, 384), f32)] * 2
                + [
                    pltpu.VMEM((32, 128), f32),
                    pltpu.VMEM((2, 8, 128), f32),
                    pltpu.SemaphoreType.DMA((12,)),
                    pltpu.SemaphoreType.DMA((12,)),
                    pltpu.SemaphoreType.DMA,
                ],
                compiler_params=pltpu.CompilerParams(
                    collective_id=0, has_side_effects=True, vmem_limit_bytes=48 << 20
                ),
            )(fields, *[jnp.asarray(m) for m in CONSTANTS])
        )

    in_specs = (P(None, "gz", "gx", "gy"),)
    out_specs = tuple([P(None, "gz", None, "gx", "gy")] * 4 + [P("gz", None, "gx", "gy")])
    return jax.shard_map(body, mesh=mesh, in_specs=in_specs, out_specs=out_specs, check_vma=False)
```

```python
import functools

import jax
import jax.numpy as jnp
import numpy as np
from jax import lax
from jax.experimental import pallas as pl
from jax.experimental.pallas import tpu as pltpu
from jax.sharding import PartitionSpec as P

MESH = pl.DeviceIdType.MESH
LEVELS = 4
NX, NY, NZ = 48, 128, 8

lift_alpha = -1.586134342059924
lift_beta = -0.052980118572961
lift_gamma = 0.882911075530934
lift_delta = 0.443506852043971
scale_low = 0.869864451624781
scale_high = 1.149604398860241


def lift_halves(even, odd, up, down):
    one = odd + lift_alpha * (even + up(even))
    two = even + lift_beta * (down(one) + one)
    three = one + lift_gamma * (two + up(two))
    four = two + lift_delta * (down(three) + three)
    return four * scale_low, three * scale_high


def operators(extent):
    tiles = 9
    line = np.zeros((tiles * extent, extent))
    line[4 * extent : 5 * extent] = np.eye(extent)
    found = []
    for level in range(LEVELS):
        low, high = lift_halves(
            line[0::2], line[1::2], lambda a: np.roll(a, -1, 0), lambda a: np.roll(a, 1, 0)
        )
        count = extent >> (level + 1)
        start = 4 * count
        pair = []
        for band in (low, high):
            rows = {}
            for k in range(band.shape[0]):
                if np.any(band[k]):
                    rows[k - start] = band[k]
            pair.append(rows)
        found.append(pair)
        line = low
    return found


ROWS_X = operators(NX)
ROWS_Y = operators(NY)
PAD_X = (24, 16, 8, 8)
PLANES = (32, 16, 8, 4)


def split_rows(pair, count):
    groups = {"own": [], "left": [], "right": [], "far": []}
    for band, rows in enumerate(pair):
        for k in sorted(rows):
            if k < -count or k >= 2 * count + 1:
                raise ValueError
            name = "left" if k < 0 else "own" if k < count else "right" if k < 2 * count else "far"
            groups[name].append((band, k, rows[k]))
    return groups


GX = [split_rows(ROWS_X[i], NX >> (i + 1)) for i in range(LEVELS)]
GY = [split_rows(ROWS_Y[i], NY >> (i + 1)) for i in range(LEVELS)]


def x_own(level):
    m = np.zeros((2 * PAD_X[level], NX), np.float32)
    for band, k, w in GX[level]["own"]:
        m[band * PAD_X[level] + k] = w
    return m


def x_edge(level):
    if level == 0:
        m = np.zeros((16, 2 * NX), np.float32)
        for side, name in enumerate(("left", "right")):
            for i, (_, _, w) in enumerate(GX[0][name]):
                for v in range(2):
                    m[8 * side + 4 * v + i, v * NX : (v + 1) * NX] = w
        return m
    m = np.zeros((16, NX), np.float32)
    for side, name in enumerate(("left", "right")):
        rows = list(GX[level][name])
        if side:
            rows = rows + GX[level]["far"]
        for i, (_, _, w) in enumerate(rows):
            m[8 * side + i] = w
    return m


def y_own(level):
    m = np.zeros((NY, 128), np.float32)
    for band, k, w in GY[level]["own"]:
        m[:, band * 64 + k] = w
    return m


def y_edge(level):
    m = np.zeros((16, NY), np.float32)
    for side, name in enumerate(("left", "right")):
        for i, (_, _, w) in enumerate(GY[level][name]):
            m[8 * side + i] = w
    return m


def y_place(level):
    count = NY >> (level + 1)
    m = np.zeros((16, 128), np.float32)
    for side, name in enumerate(("left", "right")):
        for i, (band, k, _) in enumerate(GY[level][name]):
            m[8 * side + i, band * 64 + (k + count if side == 0 else k - count)] = 1
    return m


assert not any(GY[i]["far"] for i in range(LEVELS))

def packed_table():
    parts, where, at = [], {}, 0
    for level in range(LEVELS):
        for name, m in (
            ("x_own", x_own(level)),
            ("x_edge", x_edge(level)),
            ("y_own", y_own(level)),
            ("y_edge", y_edge(level)),
            ("y_place", y_place(level)),
        ):
            wide = np.zeros((m.shape[0], 128), np.float32)
            wide[:, : m.shape[1]] = m
            parts.append(wide)
            where[name, level] = (at, m.shape)
            at += m.shape[0]
    return np.concatenate(parts), where


TABLE, WHERE = packed_table()

EDGE_AT = (0, 128, 256, 320)
EDGE_ROWS = (128, 128, 64, 32)
OWN_AT = (0, 1536, 2048, 2176)
OWN_ROWS = tuple(2 * PLANES[i] * PAD_X[i] for i in range(LEVELS))


def exact(a, b):
    return jnp.dot(a, b, precision=lax.Precision.HIGHEST, preferred_element_type=jnp.float32)


def exact_nt(a, b):
    return lax.dot_general(
        a, b, (((1,), (1,)), ((), ())), precision=lax.Precision.HIGHEST, preferred_element_type=jnp.float32
    )


def exact_tn(a, b):
    return lax.dot_general(
        a, b, (((0,), (0,)), ((), ())), precision=lax.Precision.HIGHEST, preferred_element_type=jnp.float32
    )


def stacked(wide, planes):
    return jnp.concatenate([wide[:, 128 * p : 128 * (p + 1)] for p in range(planes)], axis=0)


def kernel(ring_x, ring_y, *refs):
    fields, table_in = refs[:2]
    values = refs[2:6]
    (table, raw, wide1, wide2, wide3, wide4, m_out, c_out, k_out,
     m_in, c_in, k_in, far_m, far_k, send, recv, local) = refs[6:]
    wides = (wide1, wide2, wide3, wide4)

    def op(name, level):
        first, (rows, columns) = WHERE[name, level]
        return table[first : first + rows, :columns]

    gx, gy, gz = lax.axis_index("gx"), lax.axis_index("gy"), lax.axis_index("gz")

    def at(dx, dy):
        return (lax.rem(gx + dx + ring_x, ring_x), lax.rem(gy + dy + ring_y, ring_y), gz)

    partner = (gx, gy, 1 - gz)
    near = [(dx, dy) for dx in (-1, 0, 1) for dy in (-1, 0, 1) if dx or dy]
    barrier = pltpu.get_barrier_semaphore()
    for d in near + [(-2, -1), (-2, 0), (-2, 1)]:
        pl.semaphore_signal(barrier, inc=1, device_id=at(*d), device_id_type=MESH)
    pl.semaphore_signal(barrier, inc=1, device_id=partner, device_id_type=MESH)
    keep = pltpu.make_async_copy(fields.at[pl.ds(2 * gz, 2)], raw.at[:, pl.ds(NZ * gz, NZ)], local.at[0])
    keep.start()
    fill = pltpu.make_async_copy(table_in, table, local.at[1])
    fill.start()
    pl.semaphore_wait(barrier, 12)

    def copy(src, dst, slot, device):
        c = pltpu.make_async_remote_copy(
            src_ref=src, dst_ref=dst, send_sem=send.at[slot], recv_sem=recv.at[slot],
            device_id=device, device_id_type=MESH,
        )
        c.start()
        return c

    swap = copy(fields.at[pl.ds(2 - 2 * gz, 2)], raw.at[:, pl.ds(NZ * gz, NZ)], 0, partner)
    keep.wait()
    fill.wait()
    swap.wait()

    for v in range(2):
        planes = [raw[v, i] for i in range(2 * NZ)]
        for level in range(LEVELS):
            half = len(planes) // 2
            even, odd = planes[0::2], planes[1::2]
            one = [odd[k] + lift_alpha * (even[k] + even[(k + 1) % half]) for k in range(half)]
            two = [even[k] + lift_beta * (one[k - 1] + one[k]) for k in range(half)]
            three = [one[k] + lift_gamma * (two[k] + two[(k + 1) % half]) for k in range(half)]
            four = [two[k] + lift_delta * (three[k - 1] + three[k]) for k in range(half)]
            low = [a * scale_low for a in four]
            high = [a * scale_high for a in three]
            for i, plane in enumerate(low + high):
                if level == 0:
                    wide1[NX * v : NX * (v + 1), 128 * i : 128 * (i + 1)] = plane
                else:
                    j = v * 2 * half + i
                    wides[level][:, 128 * j : 128 * (j + 1)] = plane
            planes = low

    copies = []
    for level in range(LEVELS):
        edge = exact(op("x_edge", level), wides[level][...])
        lanes = 16 if level == 0 else PLANES[level]
        first, count = EDGE_AT[level], EDGE_ROWS[level]
        for side in range(2):
            rows = stacked(edge[8 * side : 8 * side + 8], lanes)
            m_out[side, first : first + count, :] = exact(rows, op("y_own", level))
            corner = exact_nt(op("y_edge", level), rows)
            k_out[side, :, :, first : first + count] = corner.reshape(2, 8, count)
    for side, dx in ((0, -1), (1, 1)):
        copies.append(copy(m_out.at[side], m_in.at[side], 1 + side, at(dx, 0)))
        for up, dy in ((0, -1), (1, 1)):
            copies.append(copy(k_out.at[side, up], k_in.at[side, up], 3 + 2 * side + up, at(dx, dy)))
    copies.append(copy(m_out.at[1, pl.ds(320, 32)], far_m, 7, at(2, 0)))
    for up, dy in ((0, -1), (1, 1)):
        copies.append(copy(k_out.at[1, up, :, pl.ds(256, 128)], far_k.at[up], 8 + up, at(2, dy)))

    tall = []
    for level in range(LEVELS):
        pad, p = PAD_X[level], PLANES[level]
        if level == 0:
            pieces = [exact(op("x_own", 0), wide1[NX * v : NX * (v + 1), :]) for v in range(2)]
            both = jnp.concatenate(pieces, axis=1)
        else:
            both = exact(op("x_own", level), wides[level][...])
        rows = jnp.concatenate([stacked(both[:pad], p), stacked(both[pad:], p)], axis=0)
        first, count = OWN_AT[level], OWN_ROWS[level]
        c_out[:, :, first : first + count] = exact_nt(op("y_edge", level), rows).reshape(2, 8, count)
        tall.append(rows)
    for up, dy in ((0, -1), (1, 1)):
        copies.append(copy(c_out.at[up], c_in.at[up], 10 + up, at(0, dy)))
    for level in range(LEVELS):
        pad, p = PAD_X[level], PLANES[level]
        values[level][...] = exact(tall[level], op("y_own", level)).reshape(2, p, pad, 128)

    for c in copies:
        c.wait()

    row = lax.broadcasted_iota(jnp.int32, (1, 8, 128), 1)

    def shifted(block, start, count, to):
        turn = (to - start) % 8
        if turn:
            block = pltpu.roll(block, turn, 1)
        return jnp.where((row >= to) & (row < to + count), block, 0.0)

    for level in range(LEVELS):
        pad, p = PAD_X[level], PLANES[level]
        count_x = NX >> (level + 1)
        first, count = OWN_AT[level], OWN_ROWS[level]
        c = c_in[:, :, first : first + count].reshape(16, count)
        values[level][...] += exact_tn(c, op("y_place", level)).reshape(2, p, pad, 128)
        first, count = EDGE_AT[level], EDGE_ROWS[level]
        for side in range(2):
            k = k_in[side, :, :, first : first + count].reshape(16, count)
            m = m_in[side, first : first + count, :] + exact_tn(k, op("y_place", level))
            if level == 3 and side == 1:
                k = far_k[:, :, 64:96].reshape(16, count)
                far = far_m[...] + exact_tn(k, op("y_place", level))
            block = m.reshape(count // 8, 8, 128)
            edges = GX[level]["right" if side else "left"]
            for bx in range(2):
                hits = [i for i, h in enumerate(edges) if h[0] == bx]
                k0 = edges[hits[0]][1]
                to = k0 - count_x if side else k0 + count_x
                base = to - to % 8
                if level == 0:
                    for v in range(2):
                        add = shifted(block, hits[0] + 4 * v, len(hits), to - base)
                        values[0][bx, 16 * v : 16 * v + 16, base : base + 8, :] += add
                else:
                    add = shifted(block, hits[0], len(hits), to - base)
                    if level == 3 and side == 1 and bx == 0:
                        add = add + shifted(far.reshape(count // 8, 8, 128), 6, 1, 0)
                    values[level][bx, :, base : base + 8, :] += add


def finish(*refs):
    values, outs, stages, sems = refs[:4], refs[4:9], refs[9:14], refs[14]
    copies = []
    for level in range(LEVELS):
        half = 8 >> level
        rows, columns = NX >> (level + 1), NY >> (level + 1)
        for bx in range(2):
            for by in range(2):
                for bz in range(2):
                    b = 4 * bz + 2 * by + bx
                    if b == 0 and level < 3:
                        continue
                    for v in range(2):
                        j = (2 * v + bz) * half
                        got = values[level][bx, j : j + half, :rows, 64 * by : 64 * by + columns]
                        if level == 0:
                            stages[0][b - 1, v] = got
                        else:
                            for z in range(half):
                                if b == 0:
                                    stages[4][v * rows : (v + 1) * rows, z, :] = got[z]
                                else:
                                    stages[level][b - 1, v, :, z, :] = got[z]
        copies.append(pltpu.make_async_copy(stages[level], outs[level], sems.at[level]))
        copies[-1].start()
    copies.append(pltpu.make_async_copy(stages[4], outs[4], sems.at[4]))
    copies[-1].start()
    for c in copies:
        c.wait()


def in_hbm(array):
    return pltpu.with_memory_space_constraint(array, pltpu.HBM)


def solution(mesh):
    ring_x, ring_y = mesh.shape["gx"], mesh.shape["gy"]
    shapes = [(7, 2, 8, NX >> 1, NY >> 1)]
    shapes += [(7, 2, NX >> (i + 1), 8 >> i, NY >> (i + 1)) for i in range(1, LEVELS)]
    shapes.append((2 * (NX >> LEVELS), 1, NY >> LEVELS))
    f32 = jnp.float32
    any_ = pl.BlockSpec(memory_space=pl.ANY)
    vmem = pl.BlockSpec(memory_space=pltpu.VMEM)

    def body(fields):
        values = pl.pallas_call(
            functools.partial(kernel, ring_x, ring_y),
            out_shape=[pltpu.VMEM((2, PLANES[i], PAD_X[i], 128), f32) for i in range(LEVELS)],
            in_specs=[any_] * 2,
            out_specs=[vmem] * 4,
            scratch_shapes=[
                pltpu.VMEM(TABLE.shape, f32),
                pltpu.VMEM((2, 2 * NZ, NX, NY), f32),
                pltpu.VMEM((2 * NX, 16 * NY), f32),
                pltpu.VMEM((NX, 16 * NY), f32),
                pltpu.VMEM((NX, 8 * NY), f32),
                pltpu.VMEM((NX, 4 * NY), f32),
            ]
            + [pltpu.VMEM((2, 352, 128), f32), pltpu.VMEM((2, 8, 2304), f32), pltpu.VMEM((2, 2, 8, 384), f32)] * 2
            + [
                pltpu.VMEM((32, 128), f32),
                pltpu.VMEM((2, 8, 128), f32),
                pltpu.SemaphoreType.DMA((12,)),
                pltpu.SemaphoreType.DMA((12,)),
                pltpu.SemaphoreType.DMA((2,)),
            ],
            compiler_params=pltpu.CompilerParams(
                collective_id=0, has_side_effects=True, vmem_limit_bytes=40 << 20
            ),
        )(in_hbm(fields), in_hbm(jnp.asarray(TABLE)))
        outs = pl.pallas_call(
            finish,
            out_shape=[pltpu.HBM(s, f32) for s in shapes],
            in_specs=[vmem] * 4,
            out_specs=[any_] * 5,
            scratch_shapes=[pltpu.VMEM(s, f32) for s in shapes] + [pltpu.SemaphoreType.DMA((5,))],
            compiler_params=pltpu.CompilerParams(vmem_limit_bytes=24 << 20),
        )(*values)
        small = [jnp.swapaxes(o, 2, 3) for o in outs[1:4]]
        return (outs[0], *small, outs[4].reshape(2, 1, NX >> LEVELS, NY >> LEVELS))

    in_specs = (P(None, "gz", "gx", "gy"),)
    out_specs = tuple([P(None, "gz", None, "gx", "gy")] * 4 + [P("gz", None, "gx", "gy")])
    return jax.shard_map(body, mesh=mesh, in_specs=in_specs, out_specs=out_specs, check_vma=False)
```

```python
import functools

import jax
import jax.numpy as jnp
import numpy as np
from jax import lax
from jax.experimental import pallas as pl
from jax.experimental.pallas import tpu as pltpu
from jax.sharding import PartitionSpec as P

MESH = pl.DeviceIdType.MESH
LEVELS = 4
NX, NY, NZ = 48, 128, 8

lift_alpha = -1.586134342059924
lift_beta = -0.052980118572961
lift_gamma = 0.882911075530934
lift_delta = 0.443506852043971
scale_low = 0.869864451624781
scale_high = 1.149604398860241


def lift_halves(even, odd, up, down):
    one = odd + lift_alpha * (even + up(even))
    two = even + lift_beta * (down(one) + one)
    three = one + lift_gamma * (two + up(two))
    four = two + lift_delta * (down(three) + three)
    return four * scale_low, three * scale_high


def operators(extent):
    tiles = 9
    line = np.zeros((tiles * extent, extent))
    line[4 * extent : 5 * extent] = np.eye(extent)
    found = []
    for level in range(LEVELS):
        low, high = lift_halves(
            line[0::2], line[1::2], lambda a: np.roll(a, -1, 0), lambda a: np.roll(a, 1, 0)
        )
        count = extent >> (level + 1)
        start = 4 * count
        pair = []
        for band in (low, high):
            rows = {}
            for k in range(band.shape[0]):
                if np.any(band[k]):
                    rows[k - start] = band[k]
            pair.append(rows)
        found.append(pair)
        line = low
    return found


ROWS_X = operators(NX)
ROWS_Y = operators(NY)
PAD_X = (24, 16, 8, 8)
PLANES = (32, 16, 8, 4)


def split_rows(pair, count):
    groups = {"own": [], "left": [], "right": [], "far": []}
    for band, rows in enumerate(pair):
        for k in sorted(rows):
            if k < -count or k >= 2 * count + 1:
                raise ValueError
            name = "left" if k < 0 else "own" if k < count else "right" if k < 2 * count else "far"
            groups[name].append((band, k, rows[k]))
    return groups


GX = [split_rows(ROWS_X[i], NX >> (i + 1)) for i in range(LEVELS)]
GY = [split_rows(ROWS_Y[i], NY >> (i + 1)) for i in range(LEVELS)]


def x_own(level):
    m = np.zeros((2 * PAD_X[level], NX), np.float32)
    for band, k, w in GX[level]["own"]:
        m[band * PAD_X[level] + k] = w
    return m


def x_edge(level):
    if level == 0:
        m = np.zeros((16, 2 * NX), np.float32)
        for side, name in enumerate(("left", "right")):
            for i, (_, _, w) in enumerate(GX[0][name]):
                for v in range(2):
                    m[8 * side + 4 * v + i, v * NX : (v + 1) * NX] = w
        return m
    m = np.zeros((16, NX), np.float32)
    for side, name in enumerate(("left", "right")):
        rows = list(GX[level][name])
        if side:
            rows = rows + GX[level]["far"]
        for i, (_, _, w) in enumerate(rows):
            m[8 * side + i] = w
    return m


def y_own(level):
    m = np.zeros((NY, 128), np.float32)
    for band, k, w in GY[level]["own"]:
        m[:, band * (NY >> (level + 1)) + k] = w
    return m


def y_edge(level):
    m = np.zeros((16, NY), np.float32)
    for side, name in enumerate(("left", "right")):
        for i, (_, _, w) in enumerate(GY[level][name]):
            m[8 * side + i] = w
    return m


def y_place(level):
    count = NY >> (level + 1)
    m = np.zeros((16, 128), np.float32)
    for side, name in enumerate(("left", "right")):
        for i, (band, k, _) in enumerate(GY[level][name]):
            m[8 * side + i, band * count + (k + count if side == 0 else k - count)] = 1
    return m


assert not any(GY[i]["far"] for i in range(LEVELS))

def packed_table():
    parts, where, at = [], {}, 0
    for level in range(LEVELS):
        for name, m in (
            ("x_own", x_own(level)),
            ("x_edge", x_edge(level)),
            ("y_own", y_own(level)),
            ("y_edge", y_edge(level)),
            ("y_place", y_place(level)),
        ):
            wide = np.zeros((m.shape[0], 128), np.float32)
            wide[:, : m.shape[1]] = m
            parts.append(wide)
            where[name, level] = (at, m.shape)
            at += m.shape[0]
    return np.concatenate(parts), where


TABLE, WHERE = packed_table()

EDGE_AT = (0, 128, 192, 208)
EDGE_ROWS = (128, 64, 16, 8)
EDGE_TURN = (128, 64, 32, 16)
CORNER_AT = (0, 128, 256, 320)
CORNER_ROWS = (128, 128, 64, 32)
OWN_AT = (0, 768, 1280, 1408)
OWN_ROWS = tuple(2 * PLANES[i] * PAD_X[i] for i in range(LEVELS))


def exact(a, b):
    return jnp.dot(a, b, precision=lax.Precision.HIGHEST, preferred_element_type=jnp.float32)


def exact_nt(a, b):
    return lax.dot_general(
        a, b, (((1,), (1,)), ((), ())), precision=lax.Precision.HIGHEST, preferred_element_type=jnp.float32
    )


def exact_tn(a, b):
    return lax.dot_general(
        a, b, (((0,), (0,)), ((), ())), precision=lax.Precision.HIGHEST, preferred_element_type=jnp.float32
    )


def stacked(wide, planes):
    return jnp.concatenate([wide[:, 128 * p : 128 * (p + 1)] for p in range(planes)], axis=0)


def planes_kernel(fields, table_in, table, wide1, wide2, wide3, wide4, raw, send, recv, local):
    wides = (wide1, wide2, wide3, wide4)
    gx, gy, gz = lax.axis_index("gx"), lax.axis_index("gy"), lax.axis_index("gz")
    partner = (gx, gy, 1 - gz)
    barrier = pltpu.get_barrier_semaphore()
    pl.semaphore_signal(barrier, inc=1, device_id=partner, device_id_type=MESH)
    keep = pltpu.make_async_copy(fields.at[pl.ds(2 * gz, 2)], raw.at[:, pl.ds(NZ * gz, NZ)], local.at[0])
    keep.start()
    fill = pltpu.make_async_copy(table_in, table, local.at[1])
    fill.start()
    pl.semaphore_wait(barrier, 1)
    swap = pltpu.make_async_remote_copy(
        src_ref=fields.at[pl.ds(2 - 2 * gz, 2)], dst_ref=raw.at[:, pl.ds(NZ * gz, NZ)],
        send_sem=send, recv_sem=recv, device_id=partner, device_id_type=MESH,
    )
    swap.start()
    keep.wait()
    swap.wait()
    for v in range(2):
        planes = [raw[v, i] for i in range(2 * NZ)]
        for level in range(LEVELS):
            half = len(planes) // 2
            even, odd = planes[0::2], planes[1::2]
            one = [odd[k] + lift_alpha * (even[k] + even[(k + 1) % half]) for k in range(half)]
            two = [even[k] + lift_beta * (one[k - 1] + one[k]) for k in range(half)]
            three = [one[k] + lift_gamma * (two[k] + two[(k + 1) % half]) for k in range(half)]
            four = [two[k] + lift_delta * (three[k - 1] + three[k]) for k in range(half)]
            low = [a * scale_low for a in four]
            high = [a * scale_high for a in three]
            for i, plane in enumerate(low + high):
                if level == 0:
                    wide1[NX * v : NX * (v + 1), 128 * i : 128 * (i + 1)] = plane
                else:
                    j = v * 2 * half + i
                    wides[level][:, 128 * j : 128 * (j + 1)] = plane
            planes = low
    fill.wait()


def kernel(ring_x, ring_y, *refs):
    table = refs[0]
    wides = refs[1:5]
    values = refs[5:9]
    (m_out, c_out, k_out, m_in, c_in, k_in, far_m, far_k, send, recv) = refs[9:]

    def op(name, level):
        first, (rows, columns) = WHERE[name, level]
        return table[first : first + rows, :columns]

    gx, gy, gz = lax.axis_index("gx"), lax.axis_index("gy"), lax.axis_index("gz")

    def at(dx, dy):
        return (lax.rem(gx + dx + ring_x, ring_x), lax.rem(gy + dy + ring_y, ring_y), gz)

    near = [(dx, dy) for dx in (-1, 0, 1) for dy in (-1, 0, 1) if dx or dy]
    barrier = pltpu.get_barrier_semaphore()
    for d in near + [(-2, -1), (-2, 0), (-2, 1)]:
        pl.semaphore_signal(barrier, inc=1, device_id=at(*d), device_id_type=MESH)

    def copy(src, dst, slot, device):
        c = pltpu.make_async_remote_copy(
            src_ref=src, dst_ref=dst, send_sem=send.at[slot], recv_sem=recv.at[slot],
            device_id=device, device_id_type=MESH,
        )
        c.start()
        return c

    copies = []
    for level in range(LEVELS):
        edge = exact(op("x_edge", level), wides[level][...])
        lanes = 16 if level == 0 else PLANES[level]
        first, rows = EDGE_AT[level], EDGE_ROWS[level]
        corner_at, count = CORNER_AT[level], CORNER_ROWS[level]
        both = jnp.concatenate([stacked(edge[:8], lanes), stacked(edge[8:], lanes)], axis=0)
        done = exact(both, op("y_own", level))
        corner = exact_nt(op("y_edge", level), both)
        for side in range(2):
            one = done[count * side : count * (side + 1)]
            packed = one[:rows]
            for g in range(1, count // rows):
                packed = packed + pltpu.roll(one[rows * g : rows * (g + 1)], EDGE_TURN[level] * g, 1)
            m_out[side, first : first + rows, :] = packed
            k_out[side, :, :, corner_at : corner_at + count] = corner[:, count * side : count * (side + 1)].reshape(2, 8, count)
    pl.semaphore_wait(barrier, 11)
    for side, dx in ((0, -1), (1, 1)):
        for up, dy in ((0, -1), (1, 1)):
            copies.append(copy(k_out.at[side, up], k_in.at[side, up], 2 + 2 * side + up, at(dx, dy)))
    for up, dy in ((0, -1), (1, 1)):
        copies.append(copy(k_out.at[1, up, :, pl.ds(256, 128)], far_k.at[up], 6 + up, at(2, dy)))
    copies.append(copy(m_out.at[1, pl.ds(208, 8)], far_m, 8, at(2, 0)))
    for side, dx in ((0, -1), (1, 1)):
        copies.append(copy(m_out.at[side], m_in.at[side], side, at(dx, 0)))

    tall = []
    for level in range(LEVELS):
        pad, p = PAD_X[level], PLANES[level]
        if level == 0:
            pieces = [exact(op("x_own", 0), wides[0][NX * v : NX * (v + 1), :]) for v in range(2)]
            both = jnp.concatenate(pieces, axis=1)
        else:
            both = exact(op("x_own", level), wides[level][...])
        rows = jnp.concatenate([stacked(both[:pad], p), stacked(both[pad:], p)], axis=0)
        first, count = OWN_AT[level], OWN_ROWS[level]
        c = exact_nt(op("y_edge", level), rows)
        if level == 0:
            count = count // 2
            c = c[:, :count].reshape(2, 8, count) + pltpu.roll(c[:, count:].reshape(2, 8, count), 4, 1)
        c_out[:, :, first : first + count] = c.reshape(2, 8, count)
        tall.append(rows)
    for up, dy in ((0, -1), (1, 1)):
        copies.append(copy(c_out.at[up], c_in.at[up], 9 + up, at(0, dy)))
    for level in range(LEVELS):
        pad, p = PAD_X[level], PLANES[level]
        values[level][...] = exact(tall[level], op("y_own", level)).reshape(2, p, pad, 128)

    for c in copies:
        c.wait()

    row = lax.broadcasted_iota(jnp.int32, (1, 8, 128), 1)

    def shifted(block, start, count, to):
        turn = (to - start) % 8
        if turn:
            block = pltpu.roll(block, turn, 1)
        return jnp.where((row >= to) & (row < to + count), block, 0.0)

    for level in range(LEVELS):
        pad, p = PAD_X[level], PLANES[level]
        count_x = NX >> (level + 1)
        first, count = OWN_AT[level], OWN_ROWS[level]
        if level == 0:
            c = c_in[:, :, first : first + count // 2]
            c = jnp.concatenate([c, pltpu.roll(c, 4, 1)], axis=2).reshape(16, count)
        else:
            c = c_in[:, :, first : first + count].reshape(16, count)
        values[level][...] += exact_tn(c, op("y_place", level)).reshape(2, p, pad, 128)
        first, rows = EDGE_AT[level], EDGE_ROWS[level]
        corner_at, count = CORNER_AT[level], CORNER_ROWS[level]

        def opened(packed):
            parts = [packed]
            for g in range(1, count // rows):
                parts.append(pltpu.roll(packed, 128 - EDGE_TURN[level] * g, 1))
            return jnp.concatenate(parts, axis=0)

        for side in range(2):
            k = k_in[side, :, :, corner_at : corner_at + count].reshape(16, count)
            m = opened(m_in[side, first : first + rows, :]) + exact_tn(k, op("y_place", level))
            if level == 3 and side == 1:
                k = far_k[:, :, 64:96].reshape(16, count)
                far = opened(far_m[...]) + exact_tn(k, op("y_place", level))
            block = m.reshape(count // 8, 8, 128)
            edges = GX[level]["right" if side else "left"]
            for bx in range(2):
                hits = [i for i, h in enumerate(edges) if h[0] == bx]
                k0 = edges[hits[0]][1]
                to = k0 - count_x if side else k0 + count_x
                base = to - to % 8
                if level == 0:
                    for v in range(2):
                        add = shifted(block, hits[0] + 4 * v, len(hits), to - base)
                        values[0][bx, 16 * v : 16 * v + 16, base : base + 8, :] += add
                else:
                    add = shifted(block, hits[0], len(hits), to - base)
                    if level == 3 and side == 1 and bx == 0:
                        add = add + shifted(far.reshape(count // 8, 8, 128), 6, 1, 0)
                    values[level][bx, :, base : base + 8, :] += add


def finish(*refs):
    values, outs, stages, sems = refs[:4], refs[4:9], refs[9:14], refs[14]
    copies = []
    for level in range(LEVELS):
        half = 8 >> level
        rows, columns = NX >> (level + 1), NY >> (level + 1)
        for bx in range(2):
            for by in range(2):
                for bz in range(2):
                    b = 4 * bz + 2 * by + bx
                    if b == 0 and level < 3:
                        continue
                    for v in range(2):
                        j = (2 * v + bz) * half
                        got = values[level][bx, j : j + half, :rows, columns * by : columns * (by + 1)]
                        if level == 0:
                            stages[0][b - 1, v] = got
                        else:
                            for z in range(half):
                                if b == 0:
                                    stages[4][v * rows : (v + 1) * rows, z, :] = got[z]
                                else:
                                    stages[level][b - 1, v, :, z, :] = got[z]
        copies.append(pltpu.make_async_copy(stages[level], outs[level], sems.at[level]))
        copies[-1].start()
    copies.append(pltpu.make_async_copy(stages[4], outs[4], sems.at[4]))
    copies[-1].start()
    for c in copies:
        c.wait()


def in_hbm(array):
    return pltpu.with_memory_space_constraint(array, pltpu.HBM)


def solution(mesh):
    ring_x, ring_y = mesh.shape["gx"], mesh.shape["gy"]
    shapes = [(7, 2, 8, NX >> 1, NY >> 1)]
    shapes += [(7, 2, NX >> (i + 1), 8 >> i, NY >> (i + 1)) for i in range(1, LEVELS)]
    shapes.append((2 * (NX >> LEVELS), 1, NY >> LEVELS))
    f32 = jnp.float32
    wide_shapes = [(2 * NX, 16 * NY), (NX, 16 * NY), (NX, 8 * NY), (NX, 4 * NY)]
    any_ = pl.BlockSpec(memory_space=pl.ANY)
    vmem = pl.BlockSpec(memory_space=pltpu.VMEM)

    def body(fields):
        prepared = pl.pallas_call(
            planes_kernel,
            out_shape=[pltpu.VMEM(s, f32) for s in [TABLE.shape] + wide_shapes],
            in_specs=[any_] * 2,
            out_specs=[vmem] * 5,
            scratch_shapes=[
                pltpu.VMEM((2, 2 * NZ, NX, NY), f32),
                pltpu.SemaphoreType.DMA,
                pltpu.SemaphoreType.DMA,
                pltpu.SemaphoreType.DMA((2,)),
            ],
            compiler_params=pltpu.CompilerParams(
                collective_id=1, has_side_effects=True, vmem_limit_bytes=16 << 20
            ),
        )(in_hbm(fields), in_hbm(jnp.asarray(TABLE)))
        values = pl.pallas_call(
            functools.partial(kernel, ring_x, ring_y),
            out_shape=[pltpu.VMEM((2, PLANES[i], PAD_X[i], 128), f32) for i in range(LEVELS)],
            in_specs=[vmem] * 5,
            out_specs=[vmem] * 4,
            scratch_shapes=[pltpu.VMEM((2, 216, 128), f32), pltpu.VMEM((2, 8, 1536), f32), pltpu.VMEM((2, 2, 8, 384), f32)] * 2
            + [
                pltpu.VMEM((8, 128), f32),
                pltpu.VMEM((2, 8, 128), f32),
                pltpu.SemaphoreType.DMA((11,)),
                pltpu.SemaphoreType.DMA((11,)),
            ],
            compiler_params=pltpu.CompilerParams(
                collective_id=0, has_side_effects=True, vmem_limit_bytes=40 << 20
            ),
        )(*prepared)
        outs = pl.pallas_call(
            finish,
            out_shape=[pltpu.HBM(s, f32) for s in shapes],
            in_specs=[vmem] * 4,
            out_specs=[any_] * 5,
            scratch_shapes=[pltpu.VMEM(s, f32) for s in shapes] + [pltpu.SemaphoreType.DMA((5,))],
            compiler_params=pltpu.CompilerParams(vmem_limit_bytes=24 << 20),
        )(*values)
        small = [jnp.swapaxes(o, 2, 3) for o in outs[1:4]]
        return (outs[0], *small, outs[4].reshape(2, 1, NX >> LEVELS, NY >> LEVELS))

    in_specs = (P(None, "gz", "gx", "gy"),)
    out_specs = tuple([P(None, "gz", None, "gx", "gy")] * 4 + [P("gz", None, "gx", "gy")])
    return jax.shard_map(body, mesh=mesh, in_specs=in_specs, out_specs=out_specs, check_vma=False)
```

```python
import functools

import jax
import jax.numpy as jnp
import numpy as np
from jax import lax
from jax.experimental import pallas as pl
from jax.experimental.pallas import tpu as pltpu
from jax.sharding import PartitionSpec as P

MESH = pl.DeviceIdType.MESH
LEVELS = 4
NX, NY, NZ = 48, 128, 8

lift_alpha = -1.586134342059924
lift_beta = -0.052980118572961
lift_gamma = 0.882911075530934
lift_delta = 0.443506852043971
scale_low = 0.869864451624781
scale_high = 1.149604398860241


def lift_halves(even, odd, up, down):
    one = odd + lift_alpha * (even + up(even))
    two = even + lift_beta * (down(one) + one)
    three = one + lift_gamma * (two + up(two))
    four = two + lift_delta * (down(three) + three)
    return four * scale_low, three * scale_high


def operators(extent):
    tiles = 9
    line = np.zeros((tiles * extent, extent))
    line[4 * extent : 5 * extent] = np.eye(extent)
    found = []
    for level in range(LEVELS):
        low, high = lift_halves(
            line[0::2], line[1::2], lambda a: np.roll(a, -1, 0), lambda a: np.roll(a, 1, 0)
        )
        count = extent >> (level + 1)
        start = 4 * count
        pair = []
        for band in (low, high):
            rows = {}
            for k in range(band.shape[0]):
                if np.any(band[k]):
                    rows[k - start] = band[k]
            pair.append(rows)
        found.append(pair)
        line = low
    return found


ROWS_X = operators(NX)
ROWS_Y = operators(NY)
GROUPS = 4


def split_rows(pair, count):
    groups = {"own": [], "left": [], "right": [], "far": []}
    for band, rows in enumerate(pair):
        for k in sorted(rows):
            if k < -count or k >= 2 * count + 1:
                raise ValueError
            name = "left" if k < 0 else "own" if k < count else "right" if k < 2 * count else "far"
            groups[name].append((band, k, rows[k]))
    return groups


GX = [split_rows(ROWS_X[i], NX >> (i + 1)) for i in range(LEVELS)]
GY = [split_rows(ROWS_Y[i], NY >> (i + 1)) for i in range(LEVELS)]


def depth(level):
    return 8 >> level


def band_rows(level):
    count = (NX >> (level + 1)) * (1 if level == 0 else depth(level))
    return -(-count // 8) * 8


def x_own(level):
    n = 1 if level == 0 else depth(level)
    m = np.zeros((2 * band_rows(level), n * NX), np.float32)
    for band, k, w in GX[level]["own"]:
        for z in range(n):
            m[band * band_rows(level) + k * n + z, z * NX : (z + 1) * NX] = w
    return m


def edge_base(level, side):
    return band_rows(level) - EDGE_SPAN[level] if side == 0 else 0


def x_edge(level):
    if level == 0:
        m = np.zeros((16, 2 * NX), np.float32)
        for side, name in enumerate(("left", "right")):
            for i, (_, _, w) in enumerate(GX[0][name]):
                for v in range(2):
                    m[8 * side + 4 * v + i, v * NX : (v + 1) * NX] = w
        return m
    n, span, count = depth(level), EDGE_SPAN[level], NX >> (level + 1)
    far = GX[level]["far"]
    m = np.zeros((4 * span + (8 if far else 0), n * NX), np.float32)
    for side, name in enumerate(("left", "right")):
        for band, k, w in GX[level][name]:
            for z in range(n):
                to = (k + count if side == 0 else k - count) * n + z - edge_base(level, side)
                assert 0 <= to < span
                m[(2 * side + band) * span + to, z * NX : (z + 1) * NX] = w
    for band, k, w in far:
        assert band == 0 and k == 2 * count and n == 1
        m[4 * span] = w
    return m


def y_own(level):
    m = np.zeros((NY, 128), np.float32)
    for band, k, w in GY[level]["own"]:
        m[:, band * (NY >> (level + 1)) + k] = w
    return m


def y_edge(level):
    m = np.zeros((16, NY), np.float32)
    for side, name in enumerate(("left", "right")):
        for i, (_, _, w) in enumerate(GY[level][name]):
            m[8 * side + i] = w
    return m


def y_place(level):
    count = NY >> (level + 1)
    m = np.zeros((16, 128), np.float32)
    for side, name in enumerate(("left", "right")):
        for i, (band, k, _) in enumerate(GY[level][name]):
            m[8 * side + i, band * count + (k + count if side == 0 else k - count)] = 1
    return m


assert not any(GY[i]["far"] for i in range(LEVELS))

EDGE_SPAN = (8, 16, 16, 8)


def bf16_parts(m):
    parts, rest = [], m.astype(np.float32)
    for _ in range(3):
        part = rest.astype(jnp.bfloat16)
        parts.append(part)
        rest = rest - part.astype(np.float32)
    return parts


def packed_table(names, width):
    makers = {"x_own": x_own, "x_edge": x_edge, "y_own": y_own, "y_edge": y_edge, "y_place": y_place}
    parts, where, at = [], {}, 0
    for name, level in names:
        m = makers[name](level)
        wide = np.zeros((-(-m.shape[0] // 16) * 16, width), np.float32)
        wide[: m.shape[0], : m.shape[1]] = m
        if name == "y_place":
            stacked_parts = [wide.astype(jnp.bfloat16)] * 3
        else:
            stacked_parts = bf16_parts(wide)
        parts.extend(stacked_parts)
        where[name, level] = (at, wide.shape[0], m.shape[1])
        at += 3 * wide.shape[0]
    return np.concatenate(parts), where


ALL = [(name, i) for name in ("x_own", "x_edge", "y_own", "y_edge", "y_place") for i in range(LEVELS)]
BROAD = [("x_own", 1), ("x_edge", 1)]
TABLE, WHERE = packed_table([n for n in ALL if n not in BROAD], 128)
TABLE_B, WHERE_B = packed_table(BROAD, 256)

EDGE_AT = (0, 128, 192, 224)
EDGE_ROWS = (128, 64, 32, 16)
FAR_AT, EDGE_ALL = 240, 248
EDGE_TURN = (128, 64, 32, 16)
CORNER_AT = (0, 128, 256, 384)
CORNER_ROWS = (128, 128, 128, 64)
CORNER_FAR, CORNER_ALL = 448, 512
OWN_AT = (0, 768, 1152, 1280)
OWN_ROWS = (1536,) + tuple(2 * GROUPS * band_rows(i) for i in range(1, LEVELS))
OWN_ALL = 1408


def split(a):
    high = a.astype(jnp.bfloat16)
    rest = a - high.astype(jnp.float32)
    middle = rest.astype(jnp.bfloat16)
    return high, middle, (rest - middle.astype(jnp.float32)).astype(jnp.bfloat16)


def dot(a, b, contract=((1,), (0,))):
    return lax.dot_general(a, b, (contract, ((), ())), preferred_element_type=jnp.float32)


def dot_x(operator, parts):
    n = operator.shape[0] // 3
    one, two, last = dot(operator, parts[0]), dot(operator[: 2 * n], parts[1]), dot(operator[:n], parts[2])
    return one[:n] + ((one[n : 2 * n] + two[:n]) + (one[2 * n :] + two[n:] + last))


def dot_y(rows, operator):
    high, middle, low = rows
    n = operator.shape[0] // 3
    o_high, o_middle = operator[:n], operator[n : 2 * n]
    one = dot(jnp.concatenate([high, middle], 1), jnp.concatenate([o_high, o_high], 0))
    two = dot(jnp.concatenate([low, high], 1), operator[: 2 * n])
    last = dot(jnp.concatenate([middle, high], 1), operator[n:])
    return one + (two + last)


def dot_edge(operator, rows):
    n = operator.shape[0] // 3
    contract = ((1,), (1,))
    one, two, last = dot(operator, rows[0], contract), dot(operator[: 2 * n], rows[1], contract), dot(operator[:n], rows[2], contract)
    return one[:n] + ((one[n : 2 * n] + two[:n]) + (one[2 * n :] + two[n:] + last))


def place(c, operator):
    return dot(jnp.concatenate(split(c), 0), operator, ((0,), (0,)))


def stacked(wide, planes):
    return jnp.concatenate([wide[:, 128 * p : 128 * (p + 1)] for p in range(planes)], axis=0)


def planes_kernel(fields, table_in, broad_in, table, broad, wide1, wide2, wide3, wide4, raw, send, recv, local):
    wides = (wide1, wide2, wide3, wide4)
    gx, gy, gz = lax.axis_index("gx"), lax.axis_index("gy"), lax.axis_index("gz")
    partner = (gx, gy, 1 - gz)
    barrier = pltpu.get_barrier_semaphore()
    pl.semaphore_signal(barrier, inc=1, device_id=partner, device_id_type=MESH)
    keeps = [
        pltpu.make_async_copy(fields.at[2 * gz + v], raw.at[v, pl.ds(NZ * gz, NZ)], local.at[2 + v]) for v in range(2)
    ]
    for keep in keeps:
        keep.start()
    fill = pltpu.make_async_copy(table_in, table, local.at[0])
    fill.start()
    fill_b = pltpu.make_async_copy(broad_in, broad, local.at[1])
    fill_b.start()
    pl.semaphore_wait(barrier, 1)
    swaps = [
        pltpu.make_async_remote_copy(
            src_ref=fields.at[2 - 2 * gz + v], dst_ref=raw.at[v, pl.ds(NZ * gz, NZ)],
            send_sem=send.at[v], recv_sem=recv.at[v], device_id=partner, device_id_type=MESH,
        )
        for v in range(2)
    ]
    for swap in swaps:
        swap.start()
    for v in range(2):
        keeps[v].wait()
        swaps[v].wait_recv()
        planes = [raw[v, i] for i in range(2 * NZ)]
        for level in range(LEVELS):
            half = len(planes) // 2
            even, odd = planes[0::2], planes[1::2]
            one = [odd[k] + lift_alpha * (even[k] + even[(k + 1) % half]) for k in range(half)]
            two = [even[k] + lift_beta * (one[k - 1] + one[k]) for k in range(half)]
            three = [one[k] + lift_gamma * (two[k] + two[(k + 1) % half]) for k in range(half)]
            four = [two[k] + lift_delta * (three[k - 1] + three[k]) for k in range(half)]
            low = [a * scale_low for a in four]
            high = [a * scale_high for a in three]
            for i, plane in enumerate(low + high):
                for j, part in enumerate(split(plane)):
                    if level == 0:
                        wide1[j, NX * v : NX * (v + 1), 128 * i : 128 * (i + 1)] = part
                    else:
                        g, z = 2 * v + i // half, i % half
                        wides[level][j, NX * z : NX * (z + 1), 128 * g : 128 * (g + 1)] = part
            planes = low
    fill.wait()
    fill_b.wait()
    for swap in swaps:
        swap.wait_send()


def kernel(ring_x, ring_y, *refs):
    table, broad = refs[:2]
    wides = refs[2:6]
    outs = refs[6:11]
    (v2, v3, v4, m_out, c_out, k_out, m_in, c_in, k_in, far_m, far_k, send, recv) = refs[11:]
    values = (None, v2, v3, v4)

    def op(name, level):
        if (name, level) in WHERE_B:
            first, rows, columns = WHERE_B[name, level]
            return broad[first : first + 3 * rows, :columns]
        first, rows, columns = WHERE[name, level]
        return table[first : first + 3 * rows, :columns]

    gx, gy, gz = lax.axis_index("gx"), lax.axis_index("gy"), lax.axis_index("gz")

    def at(dx, dy):
        return (lax.rem(gx + dx + ring_x, ring_x), lax.rem(gy + dy + ring_y, ring_y), gz)

    near = [(dx, dy) for dx in (-1, 0, 1) for dy in (-1, 0, 1) if dx or dy]
    barrier = pltpu.get_barrier_semaphore()
    for d in near + [(-2, -1), (-2, 0), (-2, 1)]:
        pl.semaphore_signal(barrier, inc=1, device_id=at(*d), device_id_type=MESH)

    def copy(src, dst, slot, device):
        c = pltpu.make_async_remote_copy(
            src_ref=src, dst_ref=dst, send_sem=send.at[slot], recv_sem=recv.at[slot],
            device_id=device, device_id_type=MESH,
        )
        c.start()
        return c

    copies = []
    for level in range(LEVELS):
        edge = dot_x(op("x_edge", level), wides[level])
        lanes = 16 if level == 0 else GROUPS
        first, rows = EDGE_AT[level], EDGE_ROWS[level]
        corner_at, count = CORNER_AT[level], CORNER_ROWS[level]
        per = 8 if level == 0 else 2 * EDGE_SPAN[level]
        parts = [stacked(edge[:per], lanes), stacked(edge[per : 2 * per], lanes)]
        if level == 3:
            parts.append(stacked(edge[2 * per : 2 * per + 8], lanes))
        both = jnp.concatenate(parts, axis=0)
        both = split(both)
        done = dot_y(both, op("y_own", level))
        corner = dot_edge(op("y_edge", level), both)

        def closed(block):
            n = block.shape[0] * rows // count
            packed = block[:n]
            for g in range(1, count // rows):
                packed = packed + pltpu.roll(block[n * g : n * (g + 1)], EDGE_TURN[level] * g, 1)
            return packed

        for side in range(2):
            m_out[side, first : first + rows, :] = closed(done[count * side : count * (side + 1)])
            k_out[side, :, :, corner_at : corner_at + count] = corner[:, count * side : count * (side + 1)].reshape(2, 8, count)
        if level == 3:
            m_out[1, FAR_AT:EDGE_ALL, :] = closed(done[2 * count :])
            k_out[1, :, :, CORNER_FAR : CORNER_FAR + 32] = corner[:, 2 * count :].reshape(2, 8, 32)
    pl.semaphore_wait(barrier, 11)
    for side, dx in ((0, -1), (1, 1)):
        for up, dy in ((0, -1), (1, 1)):
            copies.append(copy(k_out.at[side, up], k_in.at[side, up], 2 + 2 * side + up, at(dx, dy)))
    for up, dy in ((0, -1), (1, 1)):
        copies.append(copy(k_out.at[1, up, :, pl.ds(384, 128)], far_k.at[up], 6 + up, at(2, dy)))
    copies.append(copy(m_out.at[1, pl.ds(FAR_AT, 8)], far_m, 8, at(2, 0)))
    for side, dx in ((0, -1), (1, 1)):
        copies.append(copy(m_out.at[side, pl.ds(0, FAR_AT)], m_in.at[side, pl.ds(0, FAR_AT)], side, at(dx, 0)))

    tall = []
    for level in range(LEVELS):
        if level == 0:
            pieces = [dot_x(op("x_own", 0), wides[0].at[:, NX * v : NX * (v + 1), :]) for v in range(2)]
            rows = jnp.concatenate([stacked(p[24 * bx : 24 * (bx + 1)], 16) for bx in range(2) for p in pieces], axis=0)
        else:
            rows = stacked(dot_x(op("x_own", level), wides[level]), GROUPS)
        first, count = OWN_AT[level], OWN_ROWS[level]
        rows = split(rows)
        c = dot_edge(op("y_edge", level), rows)
        if level == 0:
            count = count // 2
            c = c[:, :count].reshape(2, 8, count) + pltpu.roll(c[:, count:].reshape(2, 8, count), 4, 1)
        c_out[:, :, first : first + count] = c.reshape(2, 8, count)
        tall.append(rows)
    y_copies = [copy(c_out.at[up], c_in.at[up], 9 + up, at(0, dy)) for up, dy in ((0, -1), (1, 1))]

    def level_one(full, add):
        for bx in range(2):
            for v in range(2):
                for bz in range(2):
                    start = ((bx * 2 + v) * 2 + bz) * 192
                    for by in range(2):
                        b = 4 * bz + 2 * by + bx
                        if b:
                            block = full[by][start : start + 192, :64].reshape(8, 24, 64)
                            if add:
                                outs[0][b - 1, v] += block
                            else:
                                outs[0][b - 1, v] = block

    full = dot_y(tall[0], op("y_own", 0))
    level_one((full, pltpu.roll(full, 64, 1)), False)
    for level in range(1, LEVELS):
        values[level][...] = dot_y(tall[level], op("y_own", level)).reshape(GROUPS, 2, band_rows(level), 128)

    for c in y_copies:
        c.wait()
    for level in range(LEVELS):
        first, count = OWN_AT[level], OWN_ROWS[level]
        if level == 0:
            c = c_in[:, :, first : first + count // 2]
            c = jnp.concatenate([c, pltpu.roll(c, 4, 1)], axis=2).reshape(16, count)
            full = place(c, op("y_place", 0))
            level_one((full, pltpu.roll(full, 64, 1)), True)
        else:
            c = c_in[:, :, first : first + count].reshape(16, count)
            values[level][...] += place(c, op("y_place", level)).reshape(GROUPS, 2, band_rows(level), 128)

    for c in copies:
        c.wait()
    row = lax.broadcasted_iota(jnp.int32, (1, 8, 128), 1)

    def shifted(block, start, count, to):
        turn = (to - start) % 8
        if turn:
            block = pltpu.roll(block, turn, 1)
        return jnp.where((row >= to) & (row < to + count), block, 0.0)

    for level in reversed(range(LEVELS)):
        first, rows = EDGE_AT[level], EDGE_ROWS[level]
        corner_at, count = CORNER_AT[level], CORNER_ROWS[level]

        def opened(packed):
            parts = [packed]
            for g in range(1, count // rows):
                parts.append(pltpu.roll(packed, 128 - EDGE_TURN[level] * g, 1))
            return jnp.concatenate(parts, axis=0)

        for side in range(2):
            k = k_in[side, :, :, corner_at : corner_at + count].reshape(16, count)
            m = opened(m_in[side, first : first + rows, :]) + place(k, op("y_place", level))
            if level:
                span, base = EDGE_SPAN[level], edge_base(level, side)
                values[level][:, :, base : base + span, :] += m.reshape(GROUPS, 2, span, 128)
                continue
            edges = GX[0]["right" if side else "left"]
            for by in range(2):
                block = (pltpu.roll(m, 64, 1) if by else m).reshape(16, 8, 128)
                for bx in range(2):
                    hits = [i for i, h in enumerate(edges) if h[0] == bx]
                    k0 = edges[hits[0]][1]
                    to = k0 - 24 if side else k0 + 24
                    base = to - to % 8
                    for v in range(2):
                        add = shifted(block, hits[0] + 4 * v, len(hits), to - base)[:, :, :64]
                        for bz in range(2):
                            b = 4 * bz + 2 * by + bx
                            if b:
                                outs[0][b - 1, v, :, base : base + 8, :] += add[8 * bz : 8 * bz + 8]
        if level == 3:
            k = far_k[:, :, 64:96].reshape(16, 32)
            far = opened(far_m[...]) + place(k, op("y_place", level))
            values[level][:, 0, 0:8, :] += far.reshape(GROUPS, 8, 128)
        if level:
            n, xs, columns = depth(level), NX >> (level + 1), NY >> (level + 1)
            for v in range(2):
                for bz in range(2):
                    for bx in range(2):
                        got = values[level][2 * v + bz, bx, : xs * n, :]
                        for by in range(2):
                            b = 4 * bz + 2 * by + bx
                            part = got[:, columns * by : columns * (by + 1)].reshape(xs, n, columns)
                            if b:
                                outs[level][b - 1, v] = part
                            elif level == 3:
                                outs[4][xs * v : xs * (v + 1)] = part


def finish(*refs):
    ins, outs, sems = refs[:5], refs[5:10], refs[10]
    copies = [pltpu.make_async_copy(ins[i], outs[i], sems.at[i]) for i in range(5)]
    for c in copies:
        c.start()
    for c in copies:
        c.wait()


def in_hbm(array):
    return pltpu.with_memory_space_constraint(array, pltpu.HBM)


def in_vmem(array):
    return pltpu.with_memory_space_constraint(array, pltpu.VMEM)


def solution(mesh):
    ring_x, ring_y = mesh.shape["gx"], mesh.shape["gy"]
    shapes = [(7, 2, 8, NX >> 1, NY >> 1)]
    shapes += [(7, 2, NX >> (i + 1), 8 >> i, NY >> (i + 1)) for i in range(1, LEVELS)]
    shapes.append((2 * (NX >> LEVELS), 1, NY >> LEVELS))
    f32 = jnp.float32
    wide_shapes = [(3, 2 * NX, 16 * NY)] + [(3, depth(i) * NX, GROUPS * NY) for i in range(1, LEVELS)]
    any_ = pl.BlockSpec(memory_space=pl.ANY)
    vmem = pl.BlockSpec(memory_space=pltpu.VMEM)

    def body(fields):
        prepared = pl.pallas_call(
            planes_kernel,
            out_shape=[pltpu.VMEM(s, jnp.bfloat16) for s in [TABLE.shape, TABLE_B.shape] + wide_shapes],
            in_specs=[any_] * 3,
            out_specs=[vmem] * 6,
            scratch_shapes=[
                pltpu.VMEM((2, 2 * NZ, NX, NY), f32),
                pltpu.SemaphoreType.DMA((2,)),
                pltpu.SemaphoreType.DMA((2,)),
                pltpu.SemaphoreType.DMA((4,)),
            ],
            compiler_params=pltpu.CompilerParams(
                collective_id=1, has_side_effects=True, vmem_limit_bytes=16 << 20
            ),
        )(in_hbm(fields), in_hbm(jnp.asarray(TABLE)), in_hbm(jnp.asarray(TABLE_B)))
        values = pl.pallas_call(
            functools.partial(kernel, ring_x, ring_y),
            out_shape=[pltpu.VMEM(s, f32) for s in shapes],
            in_specs=[vmem] * 6,
            out_specs=[vmem] * 5,
            scratch_shapes=[pltpu.VMEM((GROUPS, 2, band_rows(i), 128), f32) for i in range(1, LEVELS)]
            + [pltpu.VMEM(s, f32) for s in ((2, EDGE_ALL, 128), (2, 8, OWN_ALL), (2, 2, 8, CORNER_ALL))] * 2
            + [
                pltpu.VMEM((8, 128), f32),
                pltpu.VMEM((2, 8, 128), f32),
                pltpu.SemaphoreType.DMA((11,)),
                pltpu.SemaphoreType.DMA((11,)),
            ],
            compiler_params=pltpu.CompilerParams(
                collective_id=0, has_side_effects=True, vmem_limit_bytes=40 << 20
            ),
        )(*[in_vmem(a) for a in prepared])
        outs = pl.pallas_call(
            finish,
            out_shape=[pltpu.HBM(s, f32) for s in shapes],
            in_specs=[vmem] * 5,
            out_specs=[any_] * 5,
            scratch_shapes=[pltpu.SemaphoreType.DMA((5,))],
        )(*[in_vmem(a) for a in values])
        small = [jnp.swapaxes(o, 2, 3) for o in outs[1:4]]
        return (outs[0], *small, outs[4].reshape(2, 1, NX >> LEVELS, NY >> LEVELS))

    in_specs = (P(None, "gz", "gx", "gy"),)
    out_specs = tuple([P(None, "gz", None, "gx", "gy")] * 4 + [P("gz", None, "gx", "gy")])
    return jax.shard_map(body, mesh=mesh, in_specs=in_specs, out_specs=out_specs, check_vma=False)
```

```python
import functools

import jax
import jax.numpy as jnp
import numpy as np
from jax import lax
from jax.experimental import pallas as pl
from jax.experimental.pallas import tpu as pltpu
from jax.sharding import PartitionSpec as P

MESH = pl.DeviceIdType.MESH
LEVELS = 4
NX, NY, NZ = 48, 128, 8

lift_alpha = -1.586134342059924
lift_beta = -0.052980118572961
lift_gamma = 0.882911075530934
lift_delta = 0.443506852043971
scale_low = 0.869864451624781
scale_high = 1.149604398860241


def lift_halves(even, odd, up, down):
    one = odd + lift_alpha * (even + up(even))
    two = even + lift_beta * (down(one) + one)
    three = one + lift_gamma * (two + up(two))
    four = two + lift_delta * (down(three) + three)
    return four * scale_low, three * scale_high


def operators(extent):
    tiles = 9
    line = np.zeros((tiles * extent, extent))
    line[4 * extent : 5 * extent] = np.eye(extent)
    found = []
    for level in range(LEVELS):
        low, high = lift_halves(
            line[0::2], line[1::2], lambda a: np.roll(a, -1, 0), lambda a: np.roll(a, 1, 0)
        )
        count = extent >> (level + 1)
        start = 4 * count
        pair = []
        for band in (low, high):
            rows = {}
            for k in range(band.shape[0]):
                if np.any(band[k]):
                    rows[k - start] = band[k]
            pair.append(rows)
        found.append(pair)
        line = low
    return found


ROWS_X = operators(NX)
ROWS_Y = operators(NY)
GROUPS = 4


def split_rows(pair, count):
    groups = {"own": [], "left": [], "right": [], "far": []}
    for band, rows in enumerate(pair):
        for k in sorted(rows):
            if k < -count or k >= 2 * count + 1:
                raise ValueError
            name = "left" if k < 0 else "own" if k < count else "right" if k < 2 * count else "far"
            groups[name].append((band, k, rows[k]))
    return groups


GX = [split_rows(ROWS_X[i], NX >> (i + 1)) for i in range(LEVELS)]
GY = [split_rows(ROWS_Y[i], NY >> (i + 1)) for i in range(LEVELS)]


def depth(level):
    return 8 >> level


def band_rows(level):
    count = (NX >> (level + 1)) * (1 if level == 0 else depth(level))
    return -(-count // 8) * 8


def x_own(level):
    n = 1 if level == 0 else depth(level)
    m = np.zeros((2 * band_rows(level), n * NX), np.float32)
    for band, k, w in GX[level]["own"]:
        for z in range(n):
            m[band * band_rows(level) + k * n + z, z * NX : (z + 1) * NX] = w
    return m


def edge_base(level, side):
    return band_rows(level) - EDGE_SPAN[level] if side == 0 else 0


def x_edge(level):
    if level == 0:
        m = np.zeros((16, 2 * NX), np.float32)
        for side, name in enumerate(("left", "right")):
            for i, (_, _, w) in enumerate(GX[0][name]):
                for v in range(2):
                    m[8 * side + 4 * v + i, v * NX : (v + 1) * NX] = w
        return m
    n, span, count = depth(level), EDGE_SPAN[level], NX >> (level + 1)
    far = GX[level]["far"]
    m = np.zeros((4 * span + (8 if far else 0), n * NX), np.float32)
    for side, name in enumerate(("left", "right")):
        for band, k, w in GX[level][name]:
            for z in range(n):
                to = (k + count if side == 0 else k - count) * n + z - edge_base(level, side)
                assert 0 <= to < span
                m[(2 * side + band) * span + to, z * NX : (z + 1) * NX] = w
    for band, k, w in far:
        assert band == 0 and k == 2 * count and n == 1
        m[4 * span] = w
    return m


def y_own(level):
    m = np.zeros((NY, 128), np.float32)
    for band, k, w in GY[level]["own"]:
        m[:, band * (NY >> (level + 1)) + k] = w
    return m


def y_edge(level):
    m = np.zeros((16, NY), np.float32)
    for side, name in enumerate(("left", "right")):
        for i, (_, _, w) in enumerate(GY[level][name]):
            m[8 * side + i] = w
    return m


def y_place(level):
    count = NY >> (level + 1)
    m = np.zeros((16, 128), np.float32)
    for side, name in enumerate(("left", "right")):
        for i, (band, k, _) in enumerate(GY[level][name]):
            m[8 * side + i, band * count + (k + count if side == 0 else k - count)] = 1
    return m


assert not any(GY[i]["far"] for i in range(LEVELS))

EDGE_SPAN = (8, 16, 16, 8)


def bf16_parts(m):
    parts, rest = [], m.astype(np.float32)
    for _ in range(3):
        part = rest.astype(jnp.bfloat16)
        parts.append(part)
        rest = rest - part.astype(np.float32)
    return parts


def x_first(v):
    m = np.concatenate([x_own(0), x_edge(0)[:, v * NX : (v + 1) * NX]])
    high, middle, low = bf16_parts(m)
    none = np.zeros_like(low)
    return np.block([[high, high, high], [middle, middle, none], [low, none, none]])


def lanes_on(m):
    return np.roll(m, 64, 1)


def packed_table(names, width):
    makers = {"x_own": x_own, "x_edge": x_edge, "y_own": y_own, "y_edge": y_edge, "y_place": y_place,
              "y_high": lambda i: lanes_on(y_own(i)), "y_place_high": lambda i: lanes_on(y_place(i))}
    parts, where, at = [], {}, 0
    for name, level in names:
        m = makers[name](level)
        wide = np.zeros((-(-m.shape[0] // 16) * 16, width), np.float32)
        wide[: m.shape[0], : m.shape[1]] = m
        if name.startswith("y_place"):
            stacked_parts = [wide.astype(jnp.bfloat16)] * 3
        else:
            stacked_parts = bf16_parts(wide)
        parts.extend(stacked_parts)
        where[name, level] = (at, wide.shape[0], m.shape[1])
        at += 3 * wide.shape[0]
    return np.concatenate(parts), where


ALL = [(name, i) for name in ("x_own", "x_edge", "y_own", "y_edge", "y_place") for i in range(LEVELS)]
BROAD = [("x_own", 1), ("x_edge", 1)]
NARROW = [n for n in ALL if n not in BROAD + [("x_own", 0), ("x_edge", 0)]]
TABLE, WHERE = packed_table(NARROW + [("y_high", 0), ("y_place_high", 0)], 128)
TABLE_B, WHERE_B = packed_table(BROAD, 256)
FIRST_AT = TABLE_B.shape[0]
TABLE_B = np.concatenate([TABLE_B] + [np.pad(x_first(v), ((0, 0), (0, 256 - 3 * NX))) for v in range(2)])
FIRST_ROWS = (TABLE_B.shape[0] - FIRST_AT) // 2

EDGE_AT = (0, 128, 192, 224)
EDGE_ROWS = (128, 64, 32, 16)
FAR_AT, EDGE_ALL = 240, 248
EDGE_TURN = (128, 64, 32, 16)
CORNER_AT = (0, 128, 256, 384)
CORNER_ROWS = (128, 128, 128, 64)
CORNER_FAR, CORNER_ALL = 448, 512
OWN_AT = (0, 768, 1152, 1280)
OWN_ROWS = (1536,) + tuple(2 * GROUPS * band_rows(i) for i in range(1, LEVELS))
OWN_ALL = 1408


def split(a):
    high = a.astype(jnp.bfloat16)
    rest = a - high.astype(jnp.float32)
    middle = rest.astype(jnp.bfloat16)
    return high, middle, (rest - middle.astype(jnp.float32)).astype(jnp.bfloat16)


def dot(a, b, contract=((1,), (0,))):
    return lax.dot_general(a, b, (contract, ((), ())), preferred_element_type=jnp.float32)


def dot_x(operator, parts):
    n = operator.shape[0] // 3
    one, two, last = dot(operator, parts[0]), dot(operator[: 2 * n], parts[1]), dot(operator[:n], parts[2])
    return one[:n] + ((one[n : 2 * n] + two[:n]) + (one[2 * n :] + two[n:] + last))


def dot_y(rows, operator):
    high, middle, low = rows
    n = operator.shape[0] // 3
    o_high, o_middle = operator[:n], operator[n : 2 * n]
    one = dot(jnp.concatenate([high, middle], 1), jnp.concatenate([o_high, o_high], 0))
    two = dot(jnp.concatenate([low, high], 1), operator[: 2 * n])
    last = dot(jnp.concatenate([middle, high], 1), operator[n:])
    return one + (two + last)


def dot_edge(operator, rows):
    n = operator.shape[0] // 3
    contract = ((1,), (1,))
    one, two, last = dot(operator, rows[0], contract), dot(operator[: 2 * n], rows[1], contract), dot(operator[:n], rows[2], contract)
    return one[:n] + ((one[n : 2 * n] + two[:n]) + (one[2 * n :] + two[n:] + last))


def place(c, operator):
    return dot(jnp.concatenate(split(c), 0), operator, ((0,), (0,)))


def stacked(wide, planes):
    return jnp.concatenate([wide[:, 128 * p : 128 * (p + 1)] for p in range(planes)], axis=0)


def swap_kernel(fields, table_in, broad_in, table, broad, raw, send, recv, local):
    gx, gy, gz = lax.axis_index("gx"), lax.axis_index("gy"), lax.axis_index("gz")
    partner = (gx, gy, 1 - gz)
    barrier = pltpu.get_barrier_semaphore()
    pl.semaphore_signal(barrier, inc=1, device_id=partner, device_id_type=MESH)
    keeps = [
        pltpu.make_async_copy(fields.at[2 * gz + v], raw.at[v, pl.ds(NZ * gz, NZ)], local.at[2 + v]) for v in range(2)
    ]
    for keep in keeps:
        keep.start()
    fill = pltpu.make_async_copy(table_in, table, local.at[0])
    fill.start()
    fill_b = pltpu.make_async_copy(broad_in, broad, local.at[1])
    fill_b.start()
    pl.semaphore_wait(barrier, 1)
    swaps = [
        pltpu.make_async_remote_copy(
            src_ref=fields.at[2 - 2 * gz + v], dst_ref=raw.at[v, pl.ds(NZ * gz, NZ)],
            send_sem=send.at[v], recv_sem=recv.at[v], device_id=partner, device_id_type=MESH,
        )
        for v in range(2)
    ]
    for swap in swaps:
        swap.start()
    for v in range(2):
        keeps[v].wait()
        swaps[v].wait()
    fill.wait()
    fill_b.wait()


def kernel(ring_x, ring_y, *refs):
    table, broad, raw = refs[:3]
    outs = refs[3:8]
    (wide1, wide2, wide3, wide4, v2, v3, v4, m_out, c_out, k_out, m_in, c_in, k_in, far_m, far_k, send, recv) = refs[8:]
    wides = (wide1, wide2, wide3, wide4)
    values = (None, v2, v3, v4)

    def op(name, level):
        if (name, level) in WHERE_B:
            first, rows, columns = WHERE_B[name, level]
            return broad[first : first + 3 * rows, :columns]
        first, rows, columns = WHERE[name, level]
        return table[first : first + 3 * rows, :columns]

    gx, gy, gz = lax.axis_index("gx"), lax.axis_index("gy"), lax.axis_index("gz")

    def at(dx, dy):
        return (lax.rem(gx + dx + ring_x, ring_x), lax.rem(gy + dy + ring_y, ring_y), gz)

    near = [(dx, dy) for dx in (-1, 0, 1) for dy in (-1, 0, 1) if dx or dy]
    barrier = pltpu.get_barrier_semaphore()
    for d in near + [(-2, -1), (-2, 0), (-2, 1)]:
        pl.semaphore_signal(barrier, inc=1, device_id=at(*d), device_id_type=MESH)

    def copy(src, dst, slot, device):
        c = pltpu.make_async_remote_copy(
            src_ref=src, dst_ref=dst, send_sem=send.at[slot], recv_sem=recv.at[slot],
            device_id=device, device_id_type=MESH,
        )
        c.start()
        return c

    for v in range(2):
        planes = [raw[v, i] for i in range(2 * NZ)]
        for level in range(LEVELS):
            half = len(planes) // 2
            even, odd = planes[0::2], planes[1::2]
            one = [odd[k] + lift_alpha * (even[k] + even[(k + 1) % half]) for k in range(half)]
            two = [even[k] + lift_beta * (one[k - 1] + one[k]) for k in range(half)]
            three = [one[k] + lift_gamma * (two[k] + two[(k + 1) % half]) for k in range(half)]
            four = [two[k] + lift_delta * (three[k - 1] + three[k]) for k in range(half)]
            low = [a * scale_low for a in four]
            high = [a * scale_high for a in three]
            for i, plane in enumerate(low + high):
                for j, part in enumerate(split(plane)):
                    if level == 0:
                        wide1[v, NX * j : NX * (j + 1), 128 * i : 128 * (i + 1)] = part
                    else:
                        g, z = 2 * v + i // half, i % half
                        wides[level][j, NX * z : NX * (z + 1), 128 * g : 128 * (g + 1)] = part
            planes = low

    copies = []
    first_own, first_edge = [], 0.0
    for v in range(2):
        done = dot(broad[FIRST_AT + FIRST_ROWS * v : FIRST_AT + FIRST_ROWS * (v + 1), : 3 * NX], wide1[v])
        done = done[:64] + (done[64:128] + done[128:])
        first_own.append(done[:NX])
        first_edge = first_edge + done[NX:]
    for level in range(LEVELS):
        edge = first_edge if level == 0 else dot_x(op("x_edge", level), wides[level])
        lanes = 16 if level == 0 else GROUPS
        first, rows = EDGE_AT[level], EDGE_ROWS[level]
        corner_at, count = CORNER_AT[level], CORNER_ROWS[level]
        per = 8 if level == 0 else 2 * EDGE_SPAN[level]
        parts = [stacked(edge[:per], lanes), stacked(edge[per : 2 * per], lanes)]
        if level == 3:
            parts.append(stacked(edge[2 * per : 2 * per + 8], lanes))
        both = jnp.concatenate(parts, axis=0)
        both = split(both)
        done = dot_y(both, op("y_own", level))
        corner = dot_edge(op("y_edge", level), both)

        def closed(block):
            n = block.shape[0] * rows // count
            packed = block[:n]
            for g in range(1, count // rows):
                packed = packed + pltpu.roll(block[n * g : n * (g + 1)], EDGE_TURN[level] * g, 1)
            return packed

        for side in range(2):
            m_out[side, first : first + rows, :] = closed(done[count * side : count * (side + 1)])
            k_out[side, :, :, corner_at : corner_at + count] = corner[:, count * side : count * (side + 1)].reshape(2, 8, count)
        if level == 3:
            m_out[1, FAR_AT:EDGE_ALL, :] = closed(done[2 * count :])
            k_out[1, :, :, CORNER_FAR : CORNER_FAR + 32] = corner[:, 2 * count :].reshape(2, 8, 32)
    pl.semaphore_wait(barrier, 11)
    for side, dx in ((0, -1), (1, 1)):
        for up, dy in ((0, -1), (1, 1)):
            copies.append(copy(k_out.at[side, up], k_in.at[side, up], 2 + 2 * side + up, at(dx, dy)))
    for up, dy in ((0, -1), (1, 1)):
        copies.append(copy(k_out.at[1, up, :, pl.ds(384, 128)], far_k.at[up], 6 + up, at(2, dy)))
    copies.append(copy(m_out.at[1, pl.ds(FAR_AT, 8)], far_m, 8, at(2, 0)))
    for side, dx in ((0, -1), (1, 1)):
        copies.append(copy(m_out.at[side, pl.ds(0, FAR_AT)], m_in.at[side, pl.ds(0, FAR_AT)], side, at(dx, 0)))

    tall = []
    for level in range(LEVELS):
        if level == 0:
            rows = jnp.concatenate([stacked(p[24 * bx : 24 * (bx + 1)], 16) for bx in range(2) for p in first_own], axis=0)
        else:
            rows = stacked(dot_x(op("x_own", level), wides[level]), GROUPS)
        first, count = OWN_AT[level], OWN_ROWS[level]
        rows = split(rows)
        c = dot_edge(op("y_edge", level), rows)
        if level == 0:
            count = count // 2
            c = c[:, :count].reshape(2, 8, count) + pltpu.roll(c[:, count:].reshape(2, 8, count), 4, 1)
        c_out[:, :, first : first + count] = c.reshape(2, 8, count)
        tall.append(rows)
    y_copies = [copy(c_out.at[up], c_in.at[up], 9 + up, at(0, dy)) for up, dy in ((0, -1), (1, 1))]

    def level_one(full, add):
        for bx in range(2):
            for v in range(2):
                for bz in range(2):
                    start = ((bx * 2 + v) * 2 + bz) * 192
                    for by in range(2):
                        b = 4 * bz + 2 * by + bx
                        if b:
                            block = full[start : start + 192, 128 * by : 128 * by + 64].reshape(8, 24, 64)
                            if add:
                                outs[0][b - 1, v] += block
                            else:
                                outs[0][b - 1, v] = block

    level_one(dot_y(tall[0], jnp.concatenate([op("y_own", 0), op("y_high", 0)], 1)), False)
    for level in range(1, LEVELS):
        values[level][...] = dot_y(tall[level], op("y_own", level)).reshape(GROUPS, 2, band_rows(level), 128)

    for c in y_copies:
        c.wait()
    for level in range(LEVELS):
        first, count = OWN_AT[level], OWN_ROWS[level]
        if level == 0:
            c = c_in[:, :, first : first + count // 2]
            c = jnp.concatenate([c, pltpu.roll(c, 4, 1)], axis=2).reshape(16, count)
            level_one(place(c, jnp.concatenate([op("y_place", 0), op("y_place_high", 0)], 1)), True)
        else:
            c = c_in[:, :, first : first + count].reshape(16, count)
            values[level][...] += place(c, op("y_place", level)).reshape(GROUPS, 2, band_rows(level), 128)

    for c in copies:
        c.wait()
    row = lax.broadcasted_iota(jnp.int32, (1, 8, 128), 1)

    def shifted(block, start, count, to):
        turn = (to - start) % 8
        if turn:
            block = pltpu.roll(block, turn, 1)
        return jnp.where((row >= to) & (row < to + count), block, 0.0)

    for level in reversed(range(LEVELS)):
        first, rows = EDGE_AT[level], EDGE_ROWS[level]
        corner_at, count = CORNER_AT[level], CORNER_ROWS[level]

        def opened(packed):
            parts = [packed]
            for g in range(1, count // rows):
                parts.append(pltpu.roll(packed, 128 - EDGE_TURN[level] * g, 1))
            return jnp.concatenate(parts, axis=0)

        for side in range(2):
            k = k_in[side, :, :, corner_at : corner_at + count].reshape(16, count)
            m = opened(m_in[side, first : first + rows, :]) + place(k, op("y_place", level))
            if level:
                span, base = EDGE_SPAN[level], edge_base(level, side)
                values[level][:, :, base : base + span, :] += m.reshape(GROUPS, 2, span, 128)
                continue
            edges = GX[0]["right" if side else "left"]
            for by in range(2):
                block = (pltpu.roll(m, 64, 1) if by else m).reshape(16, 8, 128)
                for bx in range(2):
                    hits = [i for i, h in enumerate(edges) if h[0] == bx]
                    k0 = edges[hits[0]][1]
                    to = k0 - 24 if side else k0 + 24
                    base = to - to % 8
                    for v in range(2):
                        add = shifted(block, hits[0] + 4 * v, len(hits), to - base)[:, :, :64]
                        for bz in range(2):
                            b = 4 * bz + 2 * by + bx
                            if b:
                                outs[0][b - 1, v, :, base : base + 8, :] += add[8 * bz : 8 * bz + 8]
        if level == 3:
            k = far_k[:, :, 64:96].reshape(16, 32)
            far = opened(far_m[...]) + place(k, op("y_place", level))
            values[level][:, 0, 0:8, :] += far.reshape(GROUPS, 8, 128)
        if level:
            n, xs, columns = depth(level), NX >> (level + 1), NY >> (level + 1)
            for v in range(2):
                for bz in range(2):
                    for bx in range(2):
                        got = values[level][2 * v + bz, bx, : xs * n, :]
                        for by in range(2):
                            b = 4 * bz + 2 * by + bx
                            part = got[:, columns * by : columns * (by + 1)].reshape(xs, n, columns)
                            if b:
                                outs[level][b - 1, v] = part
                            elif level == 3:
                                outs[4][xs * v : xs * (v + 1)] = part


def finish(*refs):
    ins, outs, sems = refs[:5], refs[5:10], refs[10]
    copies = [pltpu.make_async_copy(ins[i], outs[i], sems.at[i]) for i in range(5)]
    for c in copies:
        c.start()
    for c in copies:
        c.wait()


def in_hbm(array):
    return pltpu.with_memory_space_constraint(array, pltpu.HBM)


def in_vmem(array):
    return pltpu.with_memory_space_constraint(array, pltpu.VMEM)


def solution(mesh):
    ring_x, ring_y = mesh.shape["gx"], mesh.shape["gy"]
    shapes = [(7, 2, 8, NX >> 1, NY >> 1)]
    shapes += [(7, 2, NX >> (i + 1), 8 >> i, NY >> (i + 1)) for i in range(1, LEVELS)]
    shapes.append((2 * (NX >> LEVELS), 1, NY >> LEVELS))
    f32 = jnp.float32
    wide_shapes = [(2, 3 * NX, 16 * NY)] + [(3, depth(i) * NX, GROUPS * NY) for i in range(1, LEVELS)]
    any_ = pl.BlockSpec(memory_space=pl.ANY)
    vmem = pl.BlockSpec(memory_space=pltpu.VMEM)

    def body(fields):
        prepared = pl.pallas_call(
            swap_kernel,
            out_shape=[pltpu.VMEM(t.shape, jnp.bfloat16) for t in (TABLE, TABLE_B)]
            + [pltpu.VMEM((2, 2 * NZ, NX, NY), f32)],
            in_specs=[any_] * 3,
            out_specs=[vmem] * 3,
            scratch_shapes=[
                pltpu.SemaphoreType.DMA((2,)),
                pltpu.SemaphoreType.DMA((2,)),
                pltpu.SemaphoreType.DMA((4,)),
            ],
            compiler_params=pltpu.CompilerParams(
                collective_id=1, has_side_effects=True, vmem_limit_bytes=16 << 20
            ),
        )(in_hbm(fields), in_hbm(jnp.asarray(TABLE)), in_hbm(jnp.asarray(TABLE_B)))
        values = pl.pallas_call(
            functools.partial(kernel, ring_x, ring_y),
            out_shape=[pltpu.VMEM(s, f32) for s in shapes],
            in_specs=[vmem] * 3,
            out_specs=[vmem] * 5,
            scratch_shapes=[pltpu.VMEM(s, jnp.bfloat16) for s in wide_shapes]
            + [pltpu.VMEM((GROUPS, 2, band_rows(i), 128), f32) for i in range(1, LEVELS)]
            + [pltpu.VMEM(s, f32) for s in ((2, EDGE_ALL, 128), (2, 8, OWN_ALL), (2, 2, 8, CORNER_ALL))] * 2
            + [
                pltpu.VMEM((8, 128), f32),
                pltpu.VMEM((2, 8, 128), f32),
                pltpu.SemaphoreType.DMA((11,)),
                pltpu.SemaphoreType.DMA((11,)),
            ],
            compiler_params=pltpu.CompilerParams(
                collective_id=0, has_side_effects=True, vmem_limit_bytes=40 << 20
            ),
        )(*[in_vmem(a) for a in prepared])
        outs = pl.pallas_call(
            finish,
            out_shape=[pltpu.HBM(s, f32) for s in shapes],
            in_specs=[vmem] * 5,
            out_specs=[any_] * 5,
            scratch_shapes=[pltpu.SemaphoreType.DMA((5,))],
        )(*[in_vmem(a) for a in values])
        small = [jnp.swapaxes(o, 2, 3) for o in outs[1:4]]
        return (outs[0], *small, outs[4].reshape(2, 1, NX >> LEVELS, NY >> LEVELS))

    in_specs = (P(None, "gz", "gx", "gy"),)
    out_specs = tuple([P(None, "gz", None, "gx", "gy")] * 4 + [P("gz", None, "gx", "gy")])
    return jax.shard_map(body, mesh=mesh, in_specs=in_specs, out_specs=out_specs, check_vma=False)
```

```python
import functools

import jax
import jax.numpy as jnp
import numpy as np
from jax import lax
from jax.experimental import pallas as pl
from jax.experimental.pallas import tpu as pltpu
from jax.sharding import PartitionSpec as P

MESH = pl.DeviceIdType.MESH
LEVELS = 4
NX, NY, NZ = 48, 128, 8

lift_alpha = -1.586134342059924
lift_beta = -0.052980118572961
lift_gamma = 0.882911075530934
lift_delta = 0.443506852043971
scale_low = 0.869864451624781
scale_high = 1.149604398860241


def lift_halves(even, odd, up, down):
    one = odd + lift_alpha * (even + up(even))
    two = even + lift_beta * (down(one) + one)
    three = one + lift_gamma * (two + up(two))
    four = two + lift_delta * (down(three) + three)
    return four * scale_low, three * scale_high


def operators(extent):
    tiles = 9
    line = np.zeros((tiles * extent, extent))
    line[4 * extent : 5 * extent] = np.eye(extent)
    found = []
    for level in range(LEVELS):
        low, high = lift_halves(
            line[0::2], line[1::2], lambda a: np.roll(a, -1, 0), lambda a: np.roll(a, 1, 0)
        )
        count = extent >> (level + 1)
        start = 4 * count
        pair = []
        for band in (low, high):
            rows = {}
            for k in range(band.shape[0]):
                if np.any(band[k]):
                    rows[k - start] = band[k]
            pair.append(rows)
        found.append(pair)
        line = low
    return found


ROWS_X = operators(NX)
ROWS_Y = operators(NY)
GROUPS = 4


def split_rows(pair, count):
    groups = {"own": [], "left": [], "right": [], "far": []}
    for band, rows in enumerate(pair):
        for k in sorted(rows):
            if k < -count or k >= 2 * count + 1:
                raise ValueError
            name = "left" if k < 0 else "own" if k < count else "right" if k < 2 * count else "far"
            groups[name].append((band, k, rows[k]))
    return groups


GX = [split_rows(ROWS_X[i], NX >> (i + 1)) for i in range(LEVELS)]
GY = [split_rows(ROWS_Y[i], NY >> (i + 1)) for i in range(LEVELS)]


def depth(level):
    return 8 >> level


def band_rows(level):
    count = (NX >> (level + 1)) * (1 if level == 0 else depth(level))
    return -(-count // 8) * 8


def x_own(level):
    n = 1 if level == 0 else depth(level)
    m = np.zeros((2 * band_rows(level), n * NX), np.float32)
    for band, k, w in GX[level]["own"]:
        for z in range(n):
            m[band * band_rows(level) + k * n + z, z * NX : (z + 1) * NX] = w
    return m


def edge_base(level, side):
    return band_rows(level) - EDGE_SPAN[level] if side == 0 else 0


def x_edge(level):
    if level == 0:
        m = np.zeros((16, 2 * NX), np.float32)
        for side, name in enumerate(("left", "right")):
            for i, (_, _, w) in enumerate(GX[0][name]):
                for v in range(2):
                    m[8 * side + 4 * v + i, v * NX : (v + 1) * NX] = w
        return m
    n, span, count = depth(level), EDGE_SPAN[level], NX >> (level + 1)
    far = GX[level]["far"]
    m = np.zeros((4 * span + (8 if far else 0), n * NX), np.float32)
    for side, name in enumerate(("left", "right")):
        for band, k, w in GX[level][name]:
            for z in range(n):
                to = (k + count if side == 0 else k - count) * n + z - edge_base(level, side)
                assert 0 <= to < span
                m[(2 * side + band) * span + to, z * NX : (z + 1) * NX] = w
    for band, k, w in far:
        assert band == 0 and k == 2 * count and n == 1
        m[4 * span] = w
    return m


def y_own(level):
    m = np.zeros((NY, 128), np.float32)
    for band, k, w in GY[level]["own"]:
        m[:, band * (NY >> (level + 1)) + k] = w
    return m


def y_edge(level):
    m = np.zeros((16, NY), np.float32)
    for side, name in enumerate(("left", "right")):
        for i, (_, _, w) in enumerate(GY[level][name]):
            m[8 * side + i] = w
    return m


def y_place(level):
    count = NY >> (level + 1)
    m = np.zeros((16, 128), np.float32)
    for side, name in enumerate(("left", "right")):
        for i, (band, k, _) in enumerate(GY[level][name]):
            m[8 * side + i, band * count + (k + count if side == 0 else k - count)] = 1
    return m


assert not any(GY[i]["far"] for i in range(LEVELS))

EDGE_SPAN = (8, 16, 16, 8)


def bf16_parts(m):
    parts, rest = [], m.astype(np.float32)
    for _ in range(3):
        part = rest.astype(jnp.bfloat16)
        parts.append(part)
        rest = rest - part.astype(np.float32)
    return parts


def x_first(v):
    m = np.concatenate([x_own(0), x_edge(0)[:, v * NX : (v + 1) * NX]])
    high, middle, low = bf16_parts(m)
    none = np.zeros_like(low)
    return np.block([[high, high, high], [middle, middle, none], [low, none, none]])


def lanes_on(m):
    return np.roll(m, 64, 1)


def packed_table(names, width):
    makers = {"x_own": x_own, "x_edge": x_edge, "y_own": y_own, "y_edge": y_edge, "y_place": y_place,
              "y_high": lambda i: lanes_on(y_own(i)), "y_place_high": lambda i: lanes_on(y_place(i))}
    parts, where, at = [], {}, 0
    for name, level in names:
        m = makers[name](level)
        wide = np.zeros((-(-m.shape[0] // 16) * 16, width), np.float32)
        wide[: m.shape[0], : m.shape[1]] = m
        if name.startswith("y_place"):
            stacked_parts = [wide.astype(jnp.bfloat16)] * 3
        else:
            stacked_parts = bf16_parts(wide)
        parts.extend(stacked_parts)
        where[name, level] = (at, wide.shape[0], m.shape[1])
        at += 3 * wide.shape[0]
    return np.concatenate(parts), where


ALL = [(name, i) for name in ("x_own", "x_edge", "y_own", "y_edge", "y_place") for i in range(LEVELS)]
BROAD = [("x_own", 1), ("x_edge", 1)]
NARROW = [n for n in ALL if n not in BROAD + [("x_own", 0), ("x_edge", 0)]]
TABLE, WHERE = packed_table(NARROW + [("y_high", 0), ("y_place_high", 0)], 128)
TABLE_B, WHERE_B = packed_table(BROAD, 256)
FIRST_AT = TABLE_B.shape[0]
TABLE_B = np.concatenate([TABLE_B] + [np.pad(x_first(v), ((0, 0), (0, 256 - 3 * NX))) for v in range(2)])
FIRST_ROWS = (TABLE_B.shape[0] - FIRST_AT) // 2

EDGE_AT = (0, 128, 192, 224)
EDGE_ROWS = (128, 64, 32, 16)
FAR_AT, EDGE_ALL = 240, 248
EDGE_TURN = (128, 64, 32, 16)
CORNER_AT = (0, 128, 256, 384)
CORNER_ROWS = (128, 128, 128, 64)
CORNER_FAR, CORNER_ALL = 448, 512
OWN_AT = (0, 768, 1152, 1280)
OWN_ROWS = (1536,) + tuple(2 * GROUPS * band_rows(i) for i in range(1, LEVELS))
OWN_ALL = 1408


def split(a):
    high = a.astype(jnp.bfloat16)
    rest = a - high.astype(jnp.float32)
    middle = rest.astype(jnp.bfloat16)
    return high, middle, (rest - middle.astype(jnp.float32)).astype(jnp.bfloat16)


def dot(a, b, contract=((1,), (0,))):
    return lax.dot_general(a, b, (contract, ((), ())), preferred_element_type=jnp.float32)


def dot_x(operator, parts):
    n = operator.shape[0] // 3
    one, two, last = dot(operator, parts[0]), dot(operator[: 2 * n], parts[1]), dot(operator[:n], parts[2])
    return one[:n] + ((one[n : 2 * n] + two[:n]) + (one[2 * n :] + two[n:] + last))


def dot_y(rows, operator):
    high, middle, low = rows
    n = operator.shape[0] // 3
    o_high, o_middle = operator[:n], operator[n : 2 * n]
    one = dot(jnp.concatenate([high, middle], 1), jnp.concatenate([o_high, o_high], 0))
    two = dot(jnp.concatenate([low, high], 1), operator[: 2 * n])
    last = dot(jnp.concatenate([middle, high], 1), operator[n:])
    return one + (two + last)


def dot_edge(operator, rows):
    n = operator.shape[0] // 3
    contract = ((1,), (1,))
    one, two, last = dot(operator, rows[0], contract), dot(operator[: 2 * n], rows[1], contract), dot(operator[:n], rows[2], contract)
    return one[:n] + ((one[n : 2 * n] + two[:n]) + (one[2 * n :] + two[n:] + last))


def place(c, operator):
    return dot(jnp.concatenate(split(c), 0), operator, ((0,), (0,)))


def stacked(wide, planes):
    return jnp.concatenate([wide[:, 128 * p : 128 * (p + 1)] for p in range(planes)], axis=0)


def swap_kernel(fields, table_in, broad_in, table, broad, raw, send, recv, local):
    gx, gy, gz = lax.axis_index("gx"), lax.axis_index("gy"), lax.axis_index("gz")
    partner = (gx, gy, 1 - gz)
    barrier = pltpu.get_barrier_semaphore()
    pl.semaphore_signal(barrier, inc=1, device_id=partner, device_id_type=MESH)
    keeps = [
        pltpu.make_async_copy(fields.at[2 * gz + v], raw.at[v, pl.ds(NZ * gz, NZ)], local.at[2 + v]) for v in range(2)
    ]
    for keep in keeps:
        keep.start()
    fill = pltpu.make_async_copy(table_in, table, local.at[0])
    fill.start()
    fill_b = pltpu.make_async_copy(broad_in, broad, local.at[1])
    fill_b.start()
    pl.semaphore_wait(barrier, 1)
    swaps = [
        pltpu.make_async_remote_copy(
            src_ref=fields.at[2 - 2 * gz + v], dst_ref=raw.at[v, pl.ds(NZ * gz, NZ)],
            send_sem=send.at[v], recv_sem=recv.at[v], device_id=partner, device_id_type=MESH,
        )
        for v in range(2)
    ]
    for swap in swaps:
        swap.start()
    for v in range(2):
        keeps[v].wait()
        swaps[v].wait()
    fill.wait()
    fill_b.wait()


def kernel(ring_x, ring_y, *refs):
    table, broad, raw = refs[:3]
    outs = refs[3:8]
    talls = refs[12:16]
    (wide1, wide2, wide3, wide4) = refs[8:12]
    (v2, v3, v4, m_out, c_out, k_out, m_in, c_in, k_in, far_m, far_k, send, recv) = refs[16:]
    wides = (wide1, wide2, wide3, wide4)
    values = (None, v2, v3, v4)

    def op(name, level):
        if (name, level) in WHERE_B:
            first, rows, columns = WHERE_B[name, level]
            return broad[first : first + 3 * rows, :columns]
        first, rows, columns = WHERE[name, level]
        return table[first : first + 3 * rows, :columns]

    gx, gy, gz = lax.axis_index("gx"), lax.axis_index("gy"), lax.axis_index("gz")

    def at(dx, dy):
        return (lax.rem(gx + dx + ring_x, ring_x), lax.rem(gy + dy + ring_y, ring_y), gz)

    near = [(dx, dy) for dx in (-1, 0, 1) for dy in (-1, 0, 1) if dx or dy]
    barrier = pltpu.get_barrier_semaphore()
    for d in near + [(-2, -1), (-2, 0), (-2, 1)]:
        pl.semaphore_signal(barrier, inc=1, device_id=at(*d), device_id_type=MESH)

    def copy(src, dst, slot, device):
        c = pltpu.make_async_remote_copy(
            src_ref=src, dst_ref=dst, send_sem=send.at[slot], recv_sem=recv.at[slot],
            device_id=device, device_id_type=MESH,
        )
        c.start()
        return c

    for v in range(2):
        planes = [raw[v, i] for i in range(2 * NZ)]
        for level in range(LEVELS):
            half = len(planes) // 2
            even, odd = planes[0::2], planes[1::2]
            one = [odd[k] + lift_alpha * (even[k] + even[(k + 1) % half]) for k in range(half)]
            two = [even[k] + lift_beta * (one[k - 1] + one[k]) for k in range(half)]
            three = [one[k] + lift_gamma * (two[k] + two[(k + 1) % half]) for k in range(half)]
            four = [two[k] + lift_delta * (three[k - 1] + three[k]) for k in range(half)]
            low = [a * scale_low for a in four]
            high = [a * scale_high for a in three]
            for i, plane in enumerate(low + high):
                for j, part in enumerate(split(plane)):
                    if level == 0:
                        wide1[v, NX * j : NX * (j + 1), 128 * i : 128 * (i + 1)] = part
                    else:
                        g, z = 2 * v + i // half, i % half
                        wides[level][j, NX * z : NX * (z + 1), 128 * g : 128 * (g + 1)] = part
            planes = low

    copies = []
    first_own, first_edge = [], 0.0
    for v in range(2):
        done = dot(broad[FIRST_AT + FIRST_ROWS * v : FIRST_AT + FIRST_ROWS * (v + 1), : 3 * NX], wide1[v])
        done = done[:64] + (done[64:128] + done[128:])
        first_own.append(done[:NX])
        first_edge = first_edge + done[NX:]
    for level in range(LEVELS):
        edge = first_edge if level == 0 else dot_x(op("x_edge", level), wides[level])
        lanes = 16 if level == 0 else GROUPS
        first, rows = EDGE_AT[level], EDGE_ROWS[level]
        corner_at, count = CORNER_AT[level], CORNER_ROWS[level]
        per = 8 if level == 0 else 2 * EDGE_SPAN[level]
        parts = [stacked(edge[:per], lanes), stacked(edge[per : 2 * per], lanes)]
        if level == 3:
            parts.append(stacked(edge[2 * per : 2 * per + 8], lanes))
        both = jnp.concatenate(parts, axis=0)
        both = split(both)
        done = dot_y(both, op("y_own", level))
        corner = dot_edge(op("y_edge", level), both)

        def closed(block):
            n = block.shape[0] * rows // count
            packed = block[:n]
            for g in range(1, count // rows):
                packed = packed + pltpu.roll(block[n * g : n * (g + 1)], EDGE_TURN[level] * g, 1)
            return packed

        for side in range(2):
            m_out[side, first : first + rows, :] = closed(done[count * side : count * (side + 1)])
            k_out[side, :, :, corner_at : corner_at + count] = corner[:, count * side : count * (side + 1)].reshape(2, 8, count)
        if level == 3:
            m_out[1, FAR_AT:EDGE_ALL, :] = closed(done[2 * count :])
            k_out[1, :, :, CORNER_FAR : CORNER_FAR + 32] = corner[:, 2 * count :].reshape(2, 8, 32)
    def own_x():
        for level in range(LEVELS):
            if level == 0:
                rows = jnp.concatenate([stacked(p[24 * bx : 24 * (bx + 1)], 16) for bx in range(2) for p in first_own], axis=0)
            else:
                rows = stacked(dot_x(op("x_own", level), wides[level]), GROUPS)
            first, count = OWN_AT[level], OWN_ROWS[level]
            rows = split(rows)
            c = dot_edge(op("y_edge", level), rows)
            if level == 0:
                count = count // 2
                c = c[:, :count].reshape(2, 8, count) + pltpu.roll(c[:, count:].reshape(2, 8, count), 4, 1)
            c_out[:, :, first : first + count] = c.reshape(2, 8, count)
            for i in range(3):
                talls[level][i] = rows[i]

    ahead = jnp.logical_or(gx == 0, gy == 0)
    pl.when(ahead)(own_x)
    pl.semaphore_wait(barrier, 11)
    for side, dx in ((0, -1), (1, 1)):
        for up, dy in ((0, -1), (1, 1)):
            copies.append(copy(k_out.at[side, up], k_in.at[side, up], 2 + 2 * side + up, at(dx, dy)))
    for up, dy in ((0, -1), (1, 1)):
        copies.append(copy(k_out.at[1, up, :, pl.ds(384, 128)], far_k.at[up], 6 + up, at(2, dy)))
    copies.append(copy(m_out.at[1, pl.ds(FAR_AT, 8)], far_m, 8, at(2, 0)))
    for side, dx in ((0, -1), (1, 1)):
        copies.append(copy(m_out.at[side, pl.ds(0, FAR_AT)], m_in.at[side, pl.ds(0, FAR_AT)], side, at(dx, 0)))

    pl.when(jnp.logical_not(ahead))(own_x)
    y_copies = [copy(c_out.at[up], c_in.at[up], 9 + up, at(0, dy)) for up, dy in ((0, -1), (1, 1))]

    def level_one(full, add):
        for bx in range(2):
            for v in range(2):
                for bz in range(2):
                    start = ((bx * 2 + v) * 2 + bz) * 192
                    for by in range(2):
                        b = 4 * bz + 2 * by + bx
                        if b:
                            block = full[start : start + 192, 128 * by : 128 * by + 64].reshape(8, 24, 64)
                            if add:
                                outs[0][b - 1, v] += block
                            else:
                                outs[0][b - 1, v] = block

    level_one(dot_y([talls[0][i] for i in range(3)], jnp.concatenate([op("y_own", 0), op("y_high", 0)], 1)), False)
    for level in range(1, LEVELS):
        values[level][...] = dot_y([talls[level][i] for i in range(3)], op("y_own", level)).reshape(GROUPS, 2, band_rows(level), 128)

    for c in y_copies:
        c.wait()
    for level in range(LEVELS):
        first, count = OWN_AT[level], OWN_ROWS[level]
        if level == 0:
            c = c_in[:, :, first : first + count // 2]
            c = jnp.concatenate([c, pltpu.roll(c, 4, 1)], axis=2).reshape(16, count)
            level_one(place(c, jnp.concatenate([op("y_place", 0), op("y_place_high", 0)], 1)), True)
        else:
            c = c_in[:, :, first : first + count].reshape(16, count)
            values[level][...] += place(c, op("y_place", level)).reshape(GROUPS, 2, band_rows(level), 128)

    for c in copies:
        c.wait()
    row = lax.broadcasted_iota(jnp.int32, (1, 8, 128), 1)

    def shifted(block, start, count, to):
        turn = (to - start) % 8
        if turn:
            block = pltpu.roll(block, turn, 1)
        return jnp.where((row >= to) & (row < to + count), block, 0.0)

    for level in reversed(range(LEVELS)):
        first, rows = EDGE_AT[level], EDGE_ROWS[level]
        corner_at, count = CORNER_AT[level], CORNER_ROWS[level]

        def opened(packed):
            parts = [packed]
            for g in range(1, count // rows):
                parts.append(pltpu.roll(packed, 128 - EDGE_TURN[level] * g, 1))
            return jnp.concatenate(parts, axis=0)

        for side in range(2):
            k = k_in[side, :, :, corner_at : corner_at + count].reshape(16, count)
            m = opened(m_in[side, first : first + rows, :]) + place(k, op("y_place", level))
            if level:
                span, base = EDGE_SPAN[level], edge_base(level, side)
                values[level][:, :, base : base + span, :] += m.reshape(GROUPS, 2, span, 128)
                continue
            edges = GX[0]["right" if side else "left"]
            for by in range(2):
                block = (pltpu.roll(m, 64, 1) if by else m).reshape(16, 8, 128)
                for bx in range(2):
                    hits = [i for i, h in enumerate(edges) if h[0] == bx]
                    k0 = edges[hits[0]][1]
                    to = k0 - 24 if side else k0 + 24
                    base = to - to % 8
                    for v in range(2):
                        add = shifted(block, hits[0] + 4 * v, len(hits), to - base)[:, :, :64]
                        for bz in range(2):
                            b = 4 * bz + 2 * by + bx
                            if b:
                                outs[0][b - 1, v, :, base : base + 8, :] += add[8 * bz : 8 * bz + 8]
        if level == 3:
            k = far_k[:, :, 64:96].reshape(16, 32)
            far = opened(far_m[...]) + place(k, op("y_place", level))
            values[level][:, 0, 0:8, :] += far.reshape(GROUPS, 8, 128)
        if level:
            n, xs, columns = depth(level), NX >> (level + 1), NY >> (level + 1)
            for v in range(2):
                for bz in range(2):
                    for bx in range(2):
                        got = values[level][2 * v + bz, bx, : xs * n, :]
                        for by in range(2):
                            b = 4 * bz + 2 * by + bx
                            part = got[:, columns * by : columns * (by + 1)].reshape(xs, n, columns)
                            if b:
                                outs[level][b - 1, v] = part
                            elif level == 3:
                                outs[4][xs * v : xs * (v + 1)] = part


def finish(*refs):
    ins, outs, sems = refs[:5], refs[5:10], refs[10]
    copies = [pltpu.make_async_copy(ins[i], outs[i], sems.at[i]) for i in range(5)]
    for c in copies:
        c.start()
    for c in copies:
        c.wait()


def in_hbm(array):
    return pltpu.with_memory_space_constraint(array, pltpu.HBM)


def in_vmem(array):
    return pltpu.with_memory_space_constraint(array, pltpu.VMEM)


def solution(mesh):
    ring_x, ring_y = mesh.shape["gx"], mesh.shape["gy"]
    shapes = [(7, 2, 8, NX >> 1, NY >> 1)]
    shapes += [(7, 2, NX >> (i + 1), 8 >> i, NY >> (i + 1)) for i in range(1, LEVELS)]
    shapes.append((2 * (NX >> LEVELS), 1, NY >> LEVELS))
    f32 = jnp.float32
    wide_shapes = [(2, 3 * NX, 16 * NY)] + [(3, depth(i) * NX, GROUPS * NY) for i in range(1, LEVELS)]
    any_ = pl.BlockSpec(memory_space=pl.ANY)
    vmem = pl.BlockSpec(memory_space=pltpu.VMEM)

    def body(fields):
        prepared = pl.pallas_call(
            swap_kernel,
            out_shape=[pltpu.VMEM(t.shape, jnp.bfloat16) for t in (TABLE, TABLE_B)]
            + [pltpu.VMEM((2, 2 * NZ, NX, NY), f32)],
            in_specs=[any_] * 3,
            out_specs=[vmem] * 3,
            scratch_shapes=[
                pltpu.SemaphoreType.DMA((2,)),
                pltpu.SemaphoreType.DMA((2,)),
                pltpu.SemaphoreType.DMA((4,)),
            ],
            compiler_params=pltpu.CompilerParams(
                collective_id=1, has_side_effects=True, vmem_limit_bytes=16 << 20
            ),
        )(in_hbm(fields), in_hbm(jnp.asarray(TABLE)), in_hbm(jnp.asarray(TABLE_B)))
        values = pl.pallas_call(
            functools.partial(kernel, ring_x, ring_y),
            out_shape=[pltpu.VMEM(s, f32) for s in shapes],
            in_specs=[vmem] * 3,
            out_specs=[vmem] * 5,
            scratch_shapes=[pltpu.VMEM(s, jnp.bfloat16) for s in wide_shapes]
            + [pltpu.VMEM((3, n, 128), jnp.bfloat16) for n in OWN_ROWS]
            + [pltpu.VMEM((GROUPS, 2, band_rows(i), 128), f32) for i in range(1, LEVELS)]
            + [pltpu.VMEM(s, f32) for s in ((2, EDGE_ALL, 128), (2, 8, OWN_ALL), (2, 2, 8, CORNER_ALL))] * 2
            + [
                pltpu.VMEM((8, 128), f32),
                pltpu.VMEM((2, 8, 128), f32),
                pltpu.SemaphoreType.DMA((11,)),
                pltpu.SemaphoreType.DMA((11,)),
            ],
            compiler_params=pltpu.CompilerParams(
                collective_id=0, has_side_effects=True, vmem_limit_bytes=40 << 20
            ),
        )(*[in_vmem(a) for a in prepared])
        outs = pl.pallas_call(
            finish,
            out_shape=[pltpu.HBM(s, f32) for s in shapes],
            in_specs=[vmem] * 5,
            out_specs=[any_] * 5,
            scratch_shapes=[pltpu.SemaphoreType.DMA((5,))],
        )(*[in_vmem(a) for a in values])
        small = [jnp.swapaxes(o, 2, 3) for o in outs[1:4]]
        return (outs[0], *small, outs[4].reshape(2, 1, NX >> LEVELS, NY >> LEVELS))

    in_specs = (P(None, "gz", "gx", "gy"),)
    out_specs = tuple([P(None, "gz", None, "gx", "gy")] * 4 + [P("gz", None, "gx", "gy")])
    return jax.shard_map(body, mesh=mesh, in_specs=in_specs, out_specs=out_specs, check_vma=False)
```

```python
import functools

import jax
import jax.numpy as jnp
import numpy as np
from jax import lax
from jax.experimental import pallas as pl
from jax.experimental.pallas import tpu as pltpu
from jax.sharding import PartitionSpec as P

MESH = pl.DeviceIdType.MESH
LEVELS = 4
NX, NY, NZ = 48, 128, 8

lift_alpha = -1.586134342059924
lift_beta = -0.052980118572961
lift_gamma = 0.882911075530934
lift_delta = 0.443506852043971
scale_low = 0.869864451624781
scale_high = 1.149604398860241


def lift_halves(even, odd, up, down):
    one = odd + lift_alpha * (even + up(even))
    two = even + lift_beta * (down(one) + one)
    three = one + lift_gamma * (two + up(two))
    four = two + lift_delta * (down(three) + three)
    return four * scale_low, three * scale_high


def operators(extent):
    tiles = 9
    line = np.zeros((tiles * extent, extent))
    line[4 * extent : 5 * extent] = np.eye(extent)
    found = []
    for level in range(LEVELS):
        low, high = lift_halves(
            line[0::2], line[1::2], lambda a: np.roll(a, -1, 0), lambda a: np.roll(a, 1, 0)
        )
        count = extent >> (level + 1)
        start = 4 * count
        pair = []
        for band in (low, high):
            rows = {}
            for k in range(band.shape[0]):
                if np.any(band[k]):
                    rows[k - start] = band[k]
            pair.append(rows)
        found.append(pair)
        line = low
    return found


ROWS_X = operators(NX)
ROWS_Y = operators(NY)
GROUPS = 4


def split_rows(pair, count):
    groups = {"own": [], "left": [], "right": [], "far": []}
    for band, rows in enumerate(pair):
        for k in sorted(rows):
            if k < -count or k >= 2 * count + 1:
                raise ValueError
            name = "left" if k < 0 else "own" if k < count else "right" if k < 2 * count else "far"
            groups[name].append((band, k, rows[k]))
    return groups


GX = [split_rows(ROWS_X[i], NX >> (i + 1)) for i in range(LEVELS)]
GY = [split_rows(ROWS_Y[i], NY >> (i + 1)) for i in range(LEVELS)]


def depth(level):
    return 8 >> level


def band_rows(level):
    count = (NX >> (level + 1)) * (1 if level == 0 else depth(level))
    return -(-count // 8) * 8


def x_own(level):
    n = 1 if level == 0 else depth(level)
    m = np.zeros((2 * band_rows(level), n * NX), np.float32)
    for band, k, w in GX[level]["own"]:
        for z in range(n):
            m[band * band_rows(level) + k * n + z, z * NX : (z + 1) * NX] = w
    return m


def edge_base(level, side):
    return band_rows(level) - EDGE_SPAN[level] if side == 0 else 0


def x_edge(level):
    if level == 0:
        m = np.zeros((16, 2 * NX), np.float32)
        for side, name in enumerate(("left", "right")):
            for i, (_, _, w) in enumerate(GX[0][name]):
                for v in range(2):
                    m[8 * side + 4 * v + i, v * NX : (v + 1) * NX] = w
        return m
    n, span, count = depth(level), EDGE_SPAN[level], NX >> (level + 1)
    far = GX[level]["far"]
    m = np.zeros((4 * span + (8 if far else 0), n * NX), np.float32)
    for side, name in enumerate(("left", "right")):
        for band, k, w in GX[level][name]:
            for z in range(n):
                to = (k + count if side == 0 else k - count) * n + z - edge_base(level, side)
                assert 0 <= to < span
                m[(2 * side + band) * span + to, z * NX : (z + 1) * NX] = w
    for band, k, w in far:
        assert band == 0 and k == 2 * count and n == 1
        m[4 * span] = w
    return m


def y_own(level):
    m = np.zeros((NY, 128), np.float32)
    for band, k, w in GY[level]["own"]:
        m[:, band * (NY >> (level + 1)) + k] = w
    return m


def y_edge(level):
    m = np.zeros((16, NY), np.float32)
    for side, name in enumerate(("left", "right")):
        for i, (_, _, w) in enumerate(GY[level][name]):
            m[8 * side + i] = w
    return m


def y_place(level):
    count = NY >> (level + 1)
    m = np.zeros((16, 128), np.float32)
    for side, name in enumerate(("left", "right")):
        for i, (band, k, _) in enumerate(GY[level][name]):
            m[8 * side + i, band * count + (k + count if side == 0 else k - count)] = 1
    return m


assert not any(GY[i]["far"] for i in range(LEVELS))

EDGE_SPAN = (8, 16, 16, 8)


def bf16_parts(m):
    parts, rest = [], m.astype(np.float32)
    for _ in range(3):
        part = rest.astype(jnp.bfloat16)
        parts.append(part)
        rest = rest - part.astype(np.float32)
    return parts


def x_first(v):
    m = np.concatenate([x_own(0), x_edge(0)[:, v * NX : (v + 1) * NX]])
    high, middle, low = bf16_parts(m)
    none = np.zeros_like(low)
    return np.block([[high, high, high], [middle, middle, none], [low, none, none]])


def lanes_on(m):
    return np.roll(m, 64, 1)


def packed_table(names, width):
    makers = {"x_own": x_own, "x_edge": x_edge, "y_own": y_own, "y_edge": y_edge, "y_place": y_place,
              "y_high": lambda i: lanes_on(y_own(i)), "y_place_high": lambda i: lanes_on(y_place(i))}
    parts, where, at = [], {}, 0
    for name, level in names:
        m = makers[name](level)
        wide = np.zeros((-(-m.shape[0] // 16) * 16, width), np.float32)
        wide[: m.shape[0], : m.shape[1]] = m
        if name.startswith("y_place"):
            stacked_parts = [wide.astype(jnp.bfloat16)] * 3
        else:
            stacked_parts = bf16_parts(wide)
        parts.extend(stacked_parts)
        where[name, level] = (at, wide.shape[0], m.shape[1])
        at += 3 * wide.shape[0]
    return np.concatenate(parts), where


ALL = [(name, i) for name in ("x_own", "x_edge", "y_own", "y_edge", "y_place") for i in range(LEVELS)]
BROAD = [("x_own", 1), ("x_edge", 1)]
NARROW = [n for n in ALL if n not in BROAD + [("x_own", 0), ("x_edge", 0)]]
TABLE, WHERE = packed_table(NARROW + [("y_high", 0), ("y_place_high", 0)], 128)
TABLE_B, WHERE_B = packed_table(BROAD, 256)
FIRST_AT = TABLE_B.shape[0]
TABLE_B = np.concatenate([TABLE_B] + [np.pad(x_first(v), ((0, 0), (0, 256 - 3 * NX))) for v in range(2)])
FIRST_ROWS = (TABLE_B.shape[0] - FIRST_AT) // 2

EDGE_AT = (0, 128, 192, 224)
EDGE_ROWS = (128, 64, 32, 16)
FAR_AT, EDGE_ALL = 240, 248
EDGE_TURN = (128, 64, 32, 16)
CORNER_AT = (0, 128, 256, 384)
CORNER_ROWS = (128, 128, 128, 64)
CORNER_FAR, CORNER_ALL = 448, 512
OWN_AT = (0, 768, 1152, 1280)
OWN_ROWS = (1536,) + tuple(2 * GROUPS * band_rows(i) for i in range(1, LEVELS))
OWN_ALL = 1408


def split(a):
    high = a.astype(jnp.bfloat16)
    rest = a - high.astype(jnp.float32)
    middle = rest.astype(jnp.bfloat16)
    return high, middle, (rest - middle.astype(jnp.float32)).astype(jnp.bfloat16)


def dot(a, b, contract=((1,), (0,))):
    return lax.dot_general(a, b, (contract, ((), ())), preferred_element_type=jnp.float32)


def dot_x(operator, parts):
    n = operator.shape[0] // 3
    one, two, last = dot(operator, parts[0]), dot(operator[: 2 * n], parts[1]), dot(operator[:n], parts[2])
    return one[:n] + ((one[n : 2 * n] + two[:n]) + (one[2 * n :] + two[n:] + last))


def dot_y(rows, operator):
    high, middle, low = rows
    n = operator.shape[0] // 3
    o_high, o_middle = operator[:n], operator[n : 2 * n]
    one = dot(jnp.concatenate([high, middle], 1), jnp.concatenate([o_high, o_high], 0))
    two = dot(jnp.concatenate([low, high], 1), operator[: 2 * n])
    last = dot(jnp.concatenate([middle, high], 1), operator[n:])
    return one + (two + last)


def dot_edge(operator, rows):
    n = operator.shape[0] // 3
    contract = ((1,), (1,))
    one, two, last = dot(operator, rows[0], contract), dot(operator[: 2 * n], rows[1], contract), dot(operator[:n], rows[2], contract)
    return one[:n] + ((one[n : 2 * n] + two[:n]) + (one[2 * n :] + two[n:] + last))


def place(c, operator):
    return dot(jnp.concatenate(split(c), 0), operator, ((0,), (0,)))


def stacked(wide, planes):
    return jnp.concatenate([wide[:, 128 * p : 128 * (p + 1)] for p in range(planes)], axis=0)


def swap_kernel(fields, table_in, broad_in, table, broad, raw, send, recv, local):
    gx, gy, gz = lax.axis_index("gx"), lax.axis_index("gy"), lax.axis_index("gz")
    partner = (gx, gy, 1 - gz)
    barrier = pltpu.get_barrier_semaphore()
    pl.semaphore_signal(barrier, inc=1, device_id=partner, device_id_type=MESH)
    keeps = [
        pltpu.make_async_copy(fields.at[2 * gz + v], raw.at[v, pl.ds(NZ * gz, NZ)], local.at[2 + v]) for v in range(2)
    ]
    for keep in keeps:
        keep.start()
    fill = pltpu.make_async_copy(table_in, table, local.at[0])
    fill.start()
    fill_b = pltpu.make_async_copy(broad_in, broad, local.at[1])
    fill_b.start()
    pl.semaphore_wait(barrier, 1)
    swaps = [
        pltpu.make_async_remote_copy(
            src_ref=fields.at[2 - 2 * gz + v], dst_ref=raw.at[v, pl.ds(NZ * gz, NZ)],
            send_sem=send.at[v], recv_sem=recv.at[v], device_id=partner, device_id_type=MESH,
        )
        for v in range(2)
    ]
    for swap in swaps:
        swap.start()
    for v in range(2):
        keeps[v].wait()
        swaps[v].wait()
    fill.wait()
    fill_b.wait()


def kernel(ring_x, ring_y, *refs):
    table, broad, raw = refs[:3]
    outs = refs[3:8]
    talls = refs[12:16]
    (wide1, wide2, wide3, wide4) = refs[8:12]
    (v2, v3, v4, m_out, c_out, k_out, m_in, c_in, k_in, far_m, far_k, send, recv) = refs[16:]
    wides = (wide1, wide2, wide3, wide4)
    values = (None, v2, v3, v4)

    def op(name, level):
        if (name, level) in WHERE_B:
            first, rows, columns = WHERE_B[name, level]
            return broad[first : first + 3 * rows, :columns]
        first, rows, columns = WHERE[name, level]
        return table[first : first + 3 * rows, :columns]

    gx, gy, gz = lax.axis_index("gx"), lax.axis_index("gy"), lax.axis_index("gz")

    def at(dx, dy):
        return (lax.rem(gx + dx + ring_x, ring_x), lax.rem(gy + dy + ring_y, ring_y), gz)

    near = [(dx, dy) for dx in (-1, 0, 1) for dy in (-1, 0, 1) if dx or dy]
    barrier = pltpu.get_barrier_semaphore()
    for d in near + [(-2, -1), (-2, 0), (-2, 1)]:
        pl.semaphore_signal(barrier, inc=1, device_id=at(*d), device_id_type=MESH)

    def copy(src, dst, slot, device):
        c = pltpu.make_async_remote_copy(
            src_ref=src, dst_ref=dst, send_sem=send.at[slot], recv_sem=recv.at[slot],
            device_id=device, device_id_type=MESH,
        )
        c.start()
        return c

    for v in range(2):
        planes = [raw[v, i] for i in range(2 * NZ)]
        for level in range(LEVELS):
            half = len(planes) // 2
            even, odd = planes[0::2], planes[1::2]
            one = [odd[k] + lift_alpha * (even[k] + even[(k + 1) % half]) for k in range(half)]
            two = [even[k] + lift_beta * (one[k - 1] + one[k]) for k in range(half)]
            three = [one[k] + lift_gamma * (two[k] + two[(k + 1) % half]) for k in range(half)]
            four = [two[k] + lift_delta * (three[k - 1] + three[k]) for k in range(half)]
            low = [a * scale_low for a in four]
            high = [a * scale_high for a in three]
            for i, plane in enumerate(low + high):
                for j, part in enumerate(split(plane)):
                    if level == 0:
                        wide1[v, NX * j : NX * (j + 1), 128 * i : 128 * (i + 1)] = part
                    else:
                        g, z = 2 * v + i // half, i % half
                        wides[level][j, NX * z : NX * (z + 1), 128 * g : 128 * (g + 1)] = part
            planes = low

    copies = []
    first_own, first_edge, edge_rows = [], 0.0, []
    for v in range(2):
        done = dot(broad[FIRST_AT + FIRST_ROWS * v : FIRST_AT + FIRST_ROWS * (v + 1), : 3 * NX], wide1[v])
        done = done[:64] + (done[64:128] + done[128:])
        first_own.append(done[:NX])
        first_edge = first_edge + done[NX:]
    for level in range(LEVELS):
        edge = first_edge if level == 0 else dot_x(op("x_edge", level), wides[level])
        lanes = 16 if level == 0 else GROUPS
        corner_at, count = CORNER_AT[level], CORNER_ROWS[level]
        per = 8 if level == 0 else 2 * EDGE_SPAN[level]
        parts = [stacked(edge[:per], lanes), stacked(edge[per : 2 * per], lanes)]
        if level == 3:
            parts.append(stacked(edge[2 * per : 2 * per + 8], lanes))
        both = jnp.concatenate(parts, axis=0)
        both = split(both)
        edge_rows.append(both)
        corner = dot_edge(op("y_edge", level), both)
        for side in range(2):
            k_out[side, :, :, corner_at : corner_at + count] = corner[:, count * side : count * (side + 1)].reshape(2, 8, count)
        if level == 3:
            k_out[1, :, :, CORNER_FAR : CORNER_FAR + 32] = corner[:, 2 * count :].reshape(2, 8, 32)

    def edges_y():
        for level in range(LEVELS):
            first, rows, count = EDGE_AT[level], EDGE_ROWS[level], CORNER_ROWS[level]
            done = dot_y(edge_rows[level], op("y_own", level))

            def closed(block):
                n = block.shape[0] * rows // count
                packed = block[:n]
                for g in range(1, count // rows):
                    packed = packed + pltpu.roll(block[n * g : n * (g + 1)], EDGE_TURN[level] * g, 1)
                return packed

            for side in range(2):
                m_out[side, first : first + rows, :] = closed(done[count * side : count * (side + 1)])
            if level == 3:
                m_out[1, FAR_AT:EDGE_ALL, :] = closed(done[2 * count :])

    def own_x():
        for level in range(LEVELS):
            if level == 0:
                rows = jnp.concatenate([stacked(p[24 * bx : 24 * (bx + 1)], 16) for bx in range(2) for p in first_own], axis=0)
            else:
                rows = stacked(dot_x(op("x_own", level), wides[level]), GROUPS)
            first, count = OWN_AT[level], OWN_ROWS[level]
            rows = split(rows)
            c = dot_edge(op("y_edge", level), rows)
            if level == 0:
                count = count // 2
                c = c[:, :count].reshape(2, 8, count) + pltpu.roll(c[:, count:].reshape(2, 8, count), 4, 1)
            c_out[:, :, first : first + count] = c.reshape(2, 8, count)
            for i in range(3):
                talls[level][i] = rows[i]

    ahead = jnp.logical_or(gx == 0, gy == 0)

    @pl.when(ahead)
    def _():
        edges_y()
        own_x()

    pl.semaphore_wait(barrier, 11)
    for side, dx in ((0, -1), (1, 1)):
        for up, dy in ((0, -1), (1, 1)):
            copies.append(copy(k_out.at[side, up], k_in.at[side, up], 2 + 2 * side + up, at(dx, dy)))
    for up, dy in ((0, -1), (1, 1)):
        copies.append(copy(k_out.at[1, up, :, pl.ds(384, 128)], far_k.at[up], 6 + up, at(2, dy)))
    pl.when(jnp.logical_not(ahead))(edges_y)
    copies.append(copy(m_out.at[1, pl.ds(FAR_AT, 8)], far_m, 8, at(2, 0)))
    for side, dx in ((0, -1), (1, 1)):
        copies.append(copy(m_out.at[side, pl.ds(0, FAR_AT)], m_in.at[side, pl.ds(0, FAR_AT)], side, at(dx, 0)))

    pl.when(jnp.logical_not(ahead))(own_x)
    y_copies = [copy(c_out.at[up], c_in.at[up], 9 + up, at(0, dy)) for up, dy in ((0, -1), (1, 1))]

    def level_one(full, add):
        for bx in range(2):
            for v in range(2):
                for bz in range(2):
                    start = ((bx * 2 + v) * 2 + bz) * 192
                    for by in range(2):
                        b = 4 * bz + 2 * by + bx
                        if b:
                            block = full[start : start + 192, 128 * by : 128 * by + 64].reshape(8, 24, 64)
                            if add:
                                outs[0][b - 1, v] += block
                            else:
                                outs[0][b - 1, v] = block

    level_one(dot_y([talls[0][i] for i in range(3)], jnp.concatenate([op("y_own", 0), op("y_high", 0)], 1)), False)
    for level in range(1, LEVELS):
        values[level][...] = dot_y([talls[level][i] for i in range(3)], op("y_own", level)).reshape(GROUPS, 2, band_rows(level), 128)

    for c in y_copies:
        c.wait()
    for level in range(LEVELS):
        first, count = OWN_AT[level], OWN_ROWS[level]
        if level == 0:
            c = c_in[:, :, first : first + count // 2]
            c = jnp.concatenate([c, pltpu.roll(c, 4, 1)], axis=2).reshape(16, count)
            level_one(place(c, jnp.concatenate([op("y_place", 0), op("y_place_high", 0)], 1)), True)
        else:
            c = c_in[:, :, first : first + count].reshape(16, count)
            values[level][...] += place(c, op("y_place", level)).reshape(GROUPS, 2, band_rows(level), 128)

    for c in copies:
        c.wait()
    row = lax.broadcasted_iota(jnp.int32, (1, 8, 128), 1)

    def shifted(block, start, count, to):
        turn = (to - start) % 8
        if turn:
            block = pltpu.roll(block, turn, 1)
        return jnp.where((row >= to) & (row < to + count), block, 0.0)

    for level in reversed(range(LEVELS)):
        first, rows = EDGE_AT[level], EDGE_ROWS[level]
        corner_at, count = CORNER_AT[level], CORNER_ROWS[level]

        def opened(packed):
            parts = [packed]
            for g in range(1, count // rows):
                parts.append(pltpu.roll(packed, 128 - EDGE_TURN[level] * g, 1))
            return jnp.concatenate(parts, axis=0)

        for side in range(2):
            k = k_in[side, :, :, corner_at : corner_at + count].reshape(16, count)
            m = opened(m_in[side, first : first + rows, :]) + place(k, op("y_place", level))
            if level:
                span, base = EDGE_SPAN[level], edge_base(level, side)
                values[level][:, :, base : base + span, :] += m.reshape(GROUPS, 2, span, 128)
                continue
            edges = GX[0]["right" if side else "left"]
            for by in range(2):
                block = (pltpu.roll(m, 64, 1) if by else m).reshape(16, 8, 128)
                for bx in range(2):
                    hits = [i for i, h in enumerate(edges) if h[0] == bx]
                    k0 = edges[hits[0]][1]
                    to = k0 - 24 if side else k0 + 24
                    base = to - to % 8
                    for v in range(2):
                        add = shifted(block, hits[0] + 4 * v, len(hits), to - base)[:, :, :64]
                        for bz in range(2):
                            b = 4 * bz + 2 * by + bx
                            if b:
                                outs[0][b - 1, v, :, base : base + 8, :] += add[8 * bz : 8 * bz + 8]
        if level == 3:
            k = far_k[:, :, 64:96].reshape(16, 32)
            far = opened(far_m[...]) + place(k, op("y_place", level))
            values[level][:, 0, 0:8, :] += far.reshape(GROUPS, 8, 128)
        if level:
            n, xs, columns = depth(level), NX >> (level + 1), NY >> (level + 1)
            for v in range(2):
                for bz in range(2):
                    for bx in range(2):
                        got = values[level][2 * v + bz, bx, : xs * n, :]
                        for by in range(2):
                            b = 4 * bz + 2 * by + bx
                            part = got[:, columns * by : columns * (by + 1)].reshape(xs, n, columns)
                            if b:
                                outs[level][b - 1, v] = part
                            elif level == 3:
                                outs[4][xs * v : xs * (v + 1)] = part


def finish(*refs):
    ins, outs, sems = refs[:5], refs[5:10], refs[10]
    copies = [pltpu.make_async_copy(ins[i], outs[i], sems.at[i]) for i in range(5)]
    for c in copies:
        c.start()
    for c in copies:
        c.wait()


def in_hbm(array):
    return pltpu.with_memory_space_constraint(array, pltpu.HBM)


def in_vmem(array):
    return pltpu.with_memory_space_constraint(array, pltpu.VMEM)


def solution(mesh):
    ring_x, ring_y = mesh.shape["gx"], mesh.shape["gy"]
    shapes = [(7, 2, 8, NX >> 1, NY >> 1)]
    shapes += [(7, 2, NX >> (i + 1), 8 >> i, NY >> (i + 1)) for i in range(1, LEVELS)]
    shapes.append((2 * (NX >> LEVELS), 1, NY >> LEVELS))
    f32 = jnp.float32
    wide_shapes = [(2, 3 * NX, 16 * NY)] + [(3, depth(i) * NX, GROUPS * NY) for i in range(1, LEVELS)]
    any_ = pl.BlockSpec(memory_space=pl.ANY)
    vmem = pl.BlockSpec(memory_space=pltpu.VMEM)

    def body(fields):
        prepared = pl.pallas_call(
            swap_kernel,
            out_shape=[pltpu.VMEM(t.shape, jnp.bfloat16) for t in (TABLE, TABLE_B)]
            + [pltpu.VMEM((2, 2 * NZ, NX, NY), f32)],
            in_specs=[any_] * 3,
            out_specs=[vmem] * 3,
            scratch_shapes=[
                pltpu.SemaphoreType.DMA((2,)),
                pltpu.SemaphoreType.DMA((2,)),
                pltpu.SemaphoreType.DMA((4,)),
            ],
            compiler_params=pltpu.CompilerParams(
                collective_id=1, has_side_effects=True, vmem_limit_bytes=16 << 20
            ),
        )(in_hbm(fields), in_hbm(jnp.asarray(TABLE)), in_hbm(jnp.asarray(TABLE_B)))
        values = pl.pallas_call(
            functools.partial(kernel, ring_x, ring_y),
            out_shape=[pltpu.VMEM(s, f32) for s in shapes],
            in_specs=[vmem] * 3,
            out_specs=[vmem] * 5,
            scratch_shapes=[pltpu.VMEM(s, jnp.bfloat16) for s in wide_shapes]
            + [pltpu.VMEM((3, n, 128), jnp.bfloat16) for n in OWN_ROWS]
            + [pltpu.VMEM((GROUPS, 2, band_rows(i), 128), f32) for i in range(1, LEVELS)]
            + [pltpu.VMEM(s, f32) for s in ((2, EDGE_ALL, 128), (2, 8, OWN_ALL), (2, 2, 8, CORNER_ALL))] * 2
            + [
                pltpu.VMEM((8, 128), f32),
                pltpu.VMEM((2, 8, 128), f32),
                pltpu.SemaphoreType.DMA((11,)),
                pltpu.SemaphoreType.DMA((11,)),
            ],
            compiler_params=pltpu.CompilerParams(
                collective_id=0, has_side_effects=True, vmem_limit_bytes=40 << 20
            ),
        )(*[in_vmem(a) for a in prepared])
        outs = pl.pallas_call(
            finish,
            out_shape=[pltpu.HBM(s, f32) for s in shapes],
            in_specs=[vmem] * 5,
            out_specs=[any_] * 5,
            scratch_shapes=[pltpu.SemaphoreType.DMA((5,))],
        )(*[in_vmem(a) for a in values])
        small = [jnp.swapaxes(o, 2, 3) for o in outs[1:4]]
        return (outs[0], *small, outs[4].reshape(2, 1, NX >> LEVELS, NY >> LEVELS))

    in_specs = (P(None, "gz", "gx", "gy"),)
    out_specs = tuple([P(None, "gz", None, "gx", "gy")] * 4 + [P("gz", None, "gx", "gy")])
    return jax.shard_map(body, mesh=mesh, in_specs=in_specs, out_specs=out_specs, check_vma=False)
```
